128 devices in a mesh: tiles: 128 (over y, x, z, core).
Axes of the slice: x: 4, y: 4, z: 4, core: 2. Of those that a mesh axis runs over, the one named last changes fastest.
Arguments:
- obs_feat: bfloat16 [262144, 256], P('tiles'), may hold values from -6 to 6
- obs_coords: float32 [3, 262144], P(None, 'tiles'), may hold values from -1 to 1
- send_rows: int32 [128, 128, 16], P('tiles'), may hold values from 0 to 2047, as said below
- send_count: int32 [128, 128], P('tiles'), may hold values from 8 to 16, as said below
- tile_id: int32 [128], P('tiles'), may hold values from 0 to 127, as said below
- cotangent: bfloat16 [524288, 512], P('tiles'), may hold values from -48 to 48
- projection: bfloat16 [256, 512], replicated, may hold values from -0.375 to 0.375
Outputs:
- grad_obs: bfloat16 [262144, 256], P('tiles')
- grad_weight: float32 [256, 512], replicated
- grad_gain: float32 [512], replicated
The draws below stay inside these ranges and needn't reach their ends.
Inputs may be any that keep to these rules, and one draw needn't show every extreme that they name: `send_rows`: entries are local rows of owner s. No row is named twice in one device's block; a row is named by at most two slots in all, and then both are live and the second lies in the block of the device whose tile is the east neighbour of the first one's tile. `send_count`: some devices hold dense tiles whose count is 16 from every owner. `tile_id`: A permutation of the tiles.
All inputs are finite; a program needn't handle non-finite values.
Results may differ from the reference program's by a relative error of at most 0.0063.
Values may be sent and summed in bfloat16 or wider, within the bound.
No kernel may reach another device: no remote copies, remote signals or barrier semaphores. Data moves between devices by JAX's collectives and lax.ppermute only.
A program may use at most 64 MiB of HBM per device.

```python
import math
import jax
import jax.numpy as jnp
from jax import lax

F = 256
C = 512
TILE_LAT = 64
TILE_LON = 64
RECV = 2048
CELLS = 4096
CAP = 16
OBS = 262144
N_TILES = 128


def layout(key):
    tile_map = jax.random.permutation(jax.random.fold_in(key, 101), N_TILES).astype(jnp.int32)
    ranking = jax.random.permutation(jax.random.fold_in(key, 102), N_TILES).astype(jnp.int32)
    dense_dest = ranking[tile_map] < max(N_TILES // 5, 1)
    edge_slots = max(CAP // 8, 1)
    sparse_counts = jax.random.randint(jax.random.fold_in(key, 103), (N_TILES, N_TILES), CAP // 2, 3 * CAP // 4 + 1).astype(jnp.int32)
    counts = jnp.where(dense_dest[None, :], jnp.int32(CAP), sparse_counts)
    owner_keys = jax.random.split(jax.random.fold_in(key, 104), N_TILES)
    orders = jax.vmap(lambda single: jax.random.permutation(single, RECV))(owner_keys).astype(jnp.int32)
    orders = orders.reshape(N_TILES, N_TILES, CAP)
    device_of = jnp.zeros((N_TILES,), jnp.int32).at[tile_map].set(jnp.arange(N_TILES, dtype=jnp.int32))
    has_west = tile_map % 16 != 0
    west_device = device_of[jnp.maximum(tile_map - 1, 0)]
    borrowed = orders[:, west_device, edge_slots:2 * edge_slots]
    leading = jnp.where(has_west[None, :, None], borrowed, orders[:, :, :edge_slots])
    slot_rows = jnp.concatenate([leading, orders[:, :, edge_slots:]], axis=2).astype(jnp.int32)
    return (tile_map, counts, orders, slot_rows, edge_slots)


def draw_tile_id(key, part):
    tile_map, counts, orders, slot_rows, edge_slots = layout(key)
    return tile_map


def draw_send_count(key, part):
    tile_map, counts, orders, slot_rows, edge_slots = layout(key)
    return counts


def draw_send_rows(key, part):
    tile_map, counts, orders, slot_rows, edge_slots = layout(key)
    return slot_rows


def draw_obs_coords(key, part):
    tile_map, counts, orders, slot_rows, edge_slots = layout(key)
    key = jax.random.fold_in(key, 7)
    shape = (N_TILES, N_TILES, CAP)
    unit_lat = jax.random.uniform(jax.random.fold_in(key, 1), shape, jnp.float32, 0.0, 1.0)
    unit_lon = jax.random.uniform(jax.random.fold_in(key, 2), shape, jnp.float32, 0.0, 1.0)
    frac_lat = unit_lat
    slot_index = jnp.arange(CAP, dtype=jnp.int32)
    edge_slot = (slot_index >= edge_slots) & (slot_index < 2 * edge_slots)
    near_east = edge_slot[None, None, :] & (tile_map % 16 != 15)[None, :, None]
    frac_lon = jnp.where(near_east, 1.0 - unit_lon / TILE_LON, unit_lon)
    lat_block = (tile_map // 16).astype(jnp.float32)[None, :, None]
    lon_block = (tile_map % 16).astype(jnp.float32)[None, :, None]
    lat = (60.0 - (lat_block + frac_lat) * TILE_LAT * 0.25) * (math.pi / 180.0)
    lon = (-120.0 + (lon_block + frac_lon) * TILE_LON * 0.25) * (math.pi / 180.0)
    vecs = jnp.stack([jnp.cos(lat) * jnp.cos(lon), jnp.cos(lat) * jnp.sin(lon), jnp.sin(lat)]).reshape(3, -1)
    columns = (jnp.arange(N_TILES, dtype=jnp.int32)[:, None, None] * RECV + orders).reshape(-1)
    return jnp.zeros((3, N_TILES * RECV), jnp.float32).at[:, columns].set(vecs)


def block_scale(stream_key, extent, shards, smallest, high):
    level, own = 1.0, jax.random.fold_in(stream_key, 6)
    for axis_at, parts in shards:
        steps = jnp.exp(jax.random.uniform(jax.random.fold_in(own, axis_at), (parts,), jnp.float32, smallest / len(shards), high / len(shards)))
        level = level * jnp.repeat(steps, extent[axis_at] // parts).reshape([-1 if axis == axis_at else 1 for axis in range(len(extent))])
    return level


def gaussian(rng, extent, width, limit, cuts=(), kind=jnp.bfloat16):
    entries = jax.random.normal(rng, extent, jnp.float32) * width
    if len(cuts) > 0:
        entries = block_scale(rng, extent, cuts, -0.22, 0.18) * entries
    return jnp.clip(entries, min=-limit, max=limit).astype(kind)


def setup_inputs(seed: int = 0) -> dict:
    keys = jax.random.split(jax.random.key(seed), 8)
    obs_feat = gaussian(keys[0], (OBS, F), 1.0, 6.0, ((0, 128),))
    obs_coords = draw_obs_coords(jax.random.fold_in(keys[7], 71), 0)
    send_rows = draw_send_rows(jax.random.fold_in(keys[7], 71), 0)
    send_count = draw_send_count(jax.random.fold_in(keys[7], 71), 0)
    tile_id = draw_tile_id(jax.random.fold_in(keys[7], 71), 0)
    cotangent = gaussian(keys[5], (N_TILES * CELLS, C), 8.0, 48.0, ((0, 128),))
    projection = gaussian(keys[6], (F, C), F ** -0.5, 0.375)
    return dict(obs_feat=obs_feat, obs_coords=obs_coords, send_rows=send_rows, send_count=send_count, tile_id=tile_id, cotangent=cotangent, projection=projection)


def cell_vectors(tile):
    lat_block = (tile // 16).astype(jnp.float32)
    lon_block = (tile % 16).astype(jnp.float32)
    row_pos = jnp.arange(TILE_LAT, dtype=jnp.float32)
    col_pos = jnp.arange(TILE_LON, dtype=jnp.float32)
    lat = (60.0 - (lat_block * TILE_LAT + row_pos + 0.5) * 0.25) * (math.pi / 180.0)
    lon = (-120.0 + (lon_block * TILE_LON + col_pos + 0.5) * 0.25) * (math.pi / 180.0)
    lat_all = jnp.broadcast_to(lat[:, None], (TILE_LAT, TILE_LON)).reshape(-1)
    lon_all = jnp.broadcast_to(lon[None, :], (TILE_LAT, TILE_LON)).reshape(-1)
    return jnp.stack([jnp.cos(lat_all) * jnp.cos(lon_all), jnp.cos(lat_all) * jnp.sin(lon_all), jnp.sin(lat_all)])

def tile_grad(cell_vecs, positions, grad_out):
    inv_width = 1.0 / (2.0 * (0.375 * math.pi / 180.0) ** 2)
    cells = cell_vecs.shape[1]
    block_len = min(cells, 1024)
    count_blocks = cells // block_len
    vec_blocks = cell_vecs.reshape(3, count_blocks, block_len).transpose(1, 0, 2)
    out_blocks = grad_out.reshape(count_blocks, block_len, grad_out.shape[1])
    channels = grad_out.shape[1]
    slots = positions.shape[1]

    def one_block(carry, pieces):
        acc_gain, acc_adj = carry
        vecs, grads = pieces
        dist = (vecs[0][:, None] - positions[0][None, :]) ** 2
        dist = dist + (vecs[1][:, None] - positions[1][None, :]) ** 2
        dist = dist + (vecs[2][:, None] - positions[2][None, :]) ** 2
        kernel = jnp.exp(-dist * inv_width)
        density = lax.optimization_barrier(jnp.sum(kernel, axis=1))
        kernel_low = kernel.astype(jnp.bfloat16)
        weighted = (grads / (1.0 + density)[:, None]).astype(jnp.bfloat16)
        acc_gain = acc_gain + lax.optimization_barrier(jnp.sum(jnp.log1p(density)[:, None] * grads, axis=0))
        acc_adj = acc_adj + lax.dot_general(kernel_low, weighted, (((0,), (0,)), ((), ())), preferred_element_type=jnp.float32)
        return ((acc_gain, acc_adj), None)
    start = (jnp.zeros((channels,), jnp.float32), jnp.zeros((slots, channels), jnp.float32))
    result, _ = lax.scan(one_block, start, (vec_blocks, out_blocks))
    return result

def reference(obs_feat, obs_coords, send_rows, send_count, tile_id, cotangent, projection):
    owners = jnp.arange(N_TILES, dtype=jnp.int32)
    slot_ids = jnp.arange(CAP, dtype=jnp.int32)

    def per_tile(carry, dest):
        acc_obs, acc_weight, acc_gain = carry
        slot_rows = lax.dynamic_index_in_dim(send_rows, dest, 1, keepdims=False)
        counts = lax.dynamic_index_in_dim(send_count, dest, 1, keepdims=False)
        live = (slot_ids[None, :] < counts[:, None]).reshape(-1)
        flat_rows = (owners[:, None] * RECV + slot_rows).reshape(-1).astype(jnp.int32)
        features = jnp.where(live[:, None], obs_feat[flat_rows], jnp.zeros((), jnp.bfloat16))
        positions = jnp.where(live[None, :], obs_coords[:, flat_rows], jnp.zeros((), jnp.float32))
        tile = lax.dynamic_index_in_dim(tile_id, dest, 0, keepdims=False)
        grad_out = lax.dynamic_slice_in_dim(cotangent, (dest * CELLS).astype(jnp.int32), CELLS, 0)
        part_gain, part_adj = tile_grad(cell_vectors(tile), positions, grad_out)
        adjoint = jnp.where(live[:, None], part_adj.astype(jnp.bfloat16), jnp.zeros((), jnp.bfloat16))
        part_weight = lax.dot_general(features, adjoint, (((0,), (0,)), ((), ())), preferred_element_type=jnp.float32)
        slot_grad = lax.dot_general(adjoint, projection, (((1,), (1,)), ((), ())), preferred_element_type=jnp.float32).astype(jnp.bfloat16)
        slot_grad = jnp.where(live[:, None], slot_grad, jnp.zeros((), jnp.bfloat16))
        acc_obs = acc_obs.at[flat_rows].add(slot_grad.astype(jnp.float32))
        return ((acc_obs, acc_weight + part_weight, acc_gain + part_gain), None)
    start = (jnp.zeros((OBS, F), jnp.float32), jnp.zeros((F, C), jnp.float32), jnp.zeros((C,), jnp.float32))
    (acc_obs, acc_weight, acc_gain), _ = lax.scan(per_tile, start, owners)
    return (acc_obs.astype(jnp.bfloat16), acc_weight * (1.0 / 256.0), acc_gain * (1.0 / 2048.0))
```

```python
import functools
import math

import jax
import jax.numpy as jnp
from jax import lax
from jax.experimental import pallas as pl
from jax.experimental.pallas import tpu as pltpu
from jax.sharding import PartitionSpec as P

f32, bf16 = jnp.float32, jnp.bfloat16
N_DEV = 128
CAP = 16
SLOTS = 2048
ROWS = 2048
FEAT = 256
CHAN = 512
CELLS = 4096
KAPPA = 1.0 / (2.0 * (0.375 * math.pi / 180.0) ** 2) / math.log(2.0)
VM = pl.BlockSpec(memory_space=pltpu.VMEM)


def call(body, out_shape, n_in, scratch=(), in_specs=None, name=None, limit=56, cost=None):
    many = isinstance(out_shape, (tuple, list))
    return pl.pallas_call(
        body,
        out_shape=out_shape,
        in_specs=in_specs or [VM] * n_in,
        out_specs=tuple(VM for _ in out_shape) if many else VM,
        scratch_shapes=list(scratch),
        compiler_params=pltpu.CompilerParams(vmem_limit_bytes=limit * 1024 * 1024),
        name=name,
        cost_estimate=cost,
    )


def cost(flops, nbytes):
    return pl.CostEstimate(flops=flops, bytes_accessed=nbytes, transcendentals=0)


def gather_pos(rl_ref, coords_ref, out_ref):
    x = coords_ref[...]
    hi = x.astype(bf16).astype(f32)
    mid = (x - hi).astype(bf16).astype(f32)
    lo = (x - hi) - mid
    parts = jnp.concatenate([hi, mid, lo, jnp.zeros((7, ROWS), f32)], axis=0).astype(bf16)
    for b in range(SLOTS // 256):
        acc = jnp.zeros((16, 256), f32)
        hot = []
        for h in range(2):
            row = rl_ref[2 * b + h : 2 * b + h + 1, :]
            iota = lax.broadcasted_iota(jnp.int32, (ROWS, 128), 0)
            hot.append(jnp.where(iota == row, 1.0, 0.0).astype(bf16))
        acc = jnp.dot(parts, jnp.concatenate(hot, axis=1), preferred_element_type=f32)
        pos = (acc[0:3] + acc[3:6]) + acc[6:9]
        for h in range(2):
            out_ref[:, 2 * b + h : 2 * b + h + 1, :] = pos[:, 128 * h : 128 * h + 128].reshape(3, 1, 128)


def gather_feat(rl_ref, feat_ref, out_ref, hot_ref):
    for b in range(4):
        for q in range(4):
            r = 4 * b + q
            col = jnp.broadcast_to(rl_ref[r : r + 1, :].astype(f32), (128, 128)).T
            lane = lax.broadcasted_iota(jnp.int32, (128, 128), 1).astype(f32)
            for t in range(ROWS // 128):
                hot_ref[128 * q : 128 * q + 128, 128 * t : 128 * t + 128] = jnp.where(
                    col - 128.0 * t == lane, 1.0, 0.0
                ).astype(bf16)
        out_ref[512 * b : 512 * b + 512, :] = jnp.dot(
            hot_ref[...], feat_ref[...], preferred_element_type=f32
        ).astype(bf16)


def adjoint_kernel(pos_ref, trig_ref, cott_ref, adjt_ref, gain_ref, v_ref, m_ref, k_ref, w_ref, dens_ref):
    cl, sl = trig_ref[0], trig_ref[1]
    cp, sp = trig_ref[2], trig_ref[3]
    for b in range(16):
        px, py, pz = pos_ref[0, b : b + 1, :], pos_ref[1, b : b + 1, :], pos_ref[2, b : b + 1, :]
        r2 = px * px + py * py
        inv = lax.rsqrt(jnp.maximum(r2, 1e-30))
        rho = r2 * inv
        cs = slice(128 * b, 128 * b + 128)
        v_ref[:, cs] = (-KAPPA * rho) * ((cl - px * inv) ** 2 + (sl - py * inv) ** 2)
        m_ref[:, cs] = -KAPPA * ((cp - rho) ** 2 + (sp - pz) ** 2)

    def group(g, _):
        base = pl.multiple_of(g * 8, 8)
        cc = trig_ref[2, pl.ds(base, 8), :]
        rows = []
        for m in range(4):
            ds = []
            for h in range(2):
                i = 2 * m + h
                c = cc[i : i + 1, :]
                d = jnp.zeros((64, 128), f32)
                for b in range(16):
                    cs = slice(128 * b, 128 * b + 128)
                    mm = m_ref[pl.ds(base, 8), cs]
                    k = jnp.exp2(c * v_ref[:, cs] + mm[i : i + 1, :])
                    d = d + k
                    k_ref[pl.ds(pl.multiple_of(g * 512, 512) + 64 * i, 64), cs] = k.astype(bf16)
                ds.append(d)
            rows.append(jnp.sum(jnp.concatenate(ds, axis=0).T, axis=0, keepdims=True))
        dens_ref[g] = jnp.concatenate(rows, axis=0)
        return 0

    lax.fori_loop(0, 8, group, 0)
    dens = dens_ref[...].reshape(32, 128)
    scale = 1.0 / (1.0 + dens)
    logd = jnp.log1p(dens)
    for r in range(4):
        rs = slice(128 * r, 128 * r + 128)
        g = jnp.zeros((128, 128), f32)
        for t in range(32):
            cs = slice(128 * t, 128 * t + 128)
            x = cott_ref[rs, cs].astype(f32)
            w_ref[rs, cs] = (x * scale[t : t + 1, :]).astype(bf16)
            g = g + x * logd[t : t + 1, :]
        gain_ref[r : r + 1, :] = jnp.sum(g.T, axis=0, keepdims=True) * (1.0 / 2048.0)

    def cols(n, _):
        cs = pl.ds(pl.multiple_of(n * 512, 512), 512)
        adjt_ref[:, cs] = jnp.dot(w_ref[...], k_ref[:, cs], preferred_element_type=f32).astype(bf16)
        return 0

    lax.fori_loop(0, SLOTS // 512, cols, 0)


def finish_tile(adjt_ref, feat_ref, proj_ref, out_ref):
    for n in range(SLOTS // 512):
        s = jnp.dot(proj_ref[...], adjt_ref[:, 512 * n : 512 * n + 512], preferred_element_type=f32)
        for h in range(2):
            t = s[128 * h : 128 * h + 128, :].T.astype(bf16)
            out_ref[8 * n : 8 * n + 8, :, 16 * h : 16 * h + 16, :] = t.reshape(8, 4, 16, 128)
    w = jnp.dot(adjt_ref[...], feat_ref[...], preferred_element_type=f32) * (1.0 / 256.0)
    for cb in range(4):
        wt = w[128 * cb : 128 * cb + 128, :].T.astype(bf16)
        out_ref[:, cb, 32:40, :] = wt.reshape(32, 8, 128)


def reduce_block(recv_ref, gain_ref, out_ref):
    total = jnp.sum(recv_ref[:, 32:40, :].astype(f32), axis=0)
    g = gain_ref[...]
    hi = g.astype(bf16).astype(f32)
    block = jnp.concatenate([total, hi, g - hi], axis=0).astype(bf16)
    out_ref[...] = jnp.broadcast_to(block[None], (N_DEV, 16, 128))


def scatter_rows(rl_ref, recv_ref, out_ref, val_ref, hot_ref):
    for h in range(2):
        val_ref[:, 128 * h : 128 * h + 128] = recv_ref[:, 16 * h : 16 * h + 16, :].reshape(SLOTS, 128)

    def rows(n, _):
        iota = lax.broadcasted_iota(jnp.int32, (512, 128), 0) + n * 512
        for b in range(16):
            hot_ref[:, 128 * b : 128 * b + 128] = jnp.where(iota == rl_ref[b : b + 1, :], 1.0, 0.0).astype(bf16)
        out_ref[pl.ds(pl.multiple_of(n * 512, 512), 512), :] = jnp.dot(
            hot_ref[...], val_ref[...], preferred_element_type=f32
        ).astype(bf16)
        return 0

    lax.fori_loop(0, ROWS // 512, rows, 0)


def assemble(x_ref, weight_ref, gain_ref):
    total = jnp.zeros((8, 128), f32)
    for cb in range(4):
        x = x_ref[:, cb].astype(f32)
        weight_ref[:, 128 * cb : 128 * cb + 128] = x[:, 0:8, :].reshape(256, 128)
        total = total + jnp.sum(x[:, 8:16, :], axis=0)
    gain_ref[...] = total[0:4] + total[4:8]


def trig_tables(tile):
    step = jnp.arange(64, dtype=f32)
    lat = (60.0 - ((tile // 16).astype(f32) * 64 + step + 0.5) * 0.25) * (math.pi / 180.0)
    lon = (-120.0 + ((tile % 16).astype(f32) * 64 + step + 0.5) * 0.25) * (math.pi / 180.0)
    t = jnp.stack([jnp.cos(lon), jnp.sin(lon), jnp.cos(lat), jnp.sin(lat)])
    return jnp.broadcast_to(t[:, :, None], (4, 64, 128))


def exchange(x):
    return lax.all_to_all(x, "tiles", split_axis=0, concat_axis=0, tiled=True)


def shards(obs_feat, obs_coords, send_rows, send_count, tile_id, cotangent, projection):
    sds = jax.ShapeDtypeStruct
    live = jnp.arange(CAP, dtype=jnp.int32)[None, :] < send_count[0][:, None]
    rl = jnp.where(live, send_rows[0], -1).reshape(16, 128)

    pos_out = call(gather_pos, sds((3, 16, 128), f32), 2, name="gather_pos")(rl, obs_coords)
    pos_out = pos_out.reshape(3, N_DEV, CAP).transpose(1, 0, 2).reshape(N_DEV, 1, 48)
    pos_out = jnp.pad(pos_out, ((0, 0), (0, 0), (0, 80)))
    pos_in = exchange(pos_out)[:, 0, :48]
    pos = pos_in.reshape(N_DEV, 3, CAP).transpose(1, 0, 2).reshape(3, 16, 128)

    feat_out = call(
        gather_feat, sds((SLOTS, FEAT), bf16), 2, scratch=[pltpu.VMEM((512, ROWS), bf16)], name="gather_feat",
        cost=cost(4 * 10**9, 2 * 2**20),
    )(rl, obs_feat)
    cott = cotangent.T
    trig = trig_tables(tile_id[0])

    feat_in = exchange(feat_out.reshape(N_DEV, CAP, FEAT)).reshape(SLOTS, FEAT)
    adjt, gain = call(
        adjoint_kernel,
        (sds((CHAN, SLOTS), bf16), sds((4, 128), f32)),
        3,
        scratch=[
            pltpu.VMEM((64, SLOTS), f32),
            pltpu.VMEM((64, SLOTS), f32),
            pltpu.VMEM((CELLS, SLOTS), bf16),
            pltpu.VMEM((CHAN, CELLS), bf16),
            pltpu.VMEM((8, 4, 128), f32),
        ],
        name="adjoint",
        cost=cost(20 * 10**9, 8 * 2**20),
    )(pos, trig, cott)

    out = call(finish_tile, sds((32, 4, 40, 128), bf16), 3, name="finish_tile")(adjt, feat_in, projection)
    recv = exchange(out.reshape(N_DEV, 40, 128))
    block = call(reduce_block, sds((N_DEV, 16, 128), bf16), 2, name="reduce_block")(recv, gain)
    blocks = exchange(block)
    grad_obs = call(
        scatter_rows,
        sds((ROWS, FEAT), bf16),
        2,
        scratch=[pltpu.VMEM((SLOTS, FEAT), bf16), pltpu.VMEM((512, SLOTS), bf16)],
        name="scatter_rows",
        cost=cost(4 * 10**9, 3 * 2**20),
    )(rl, recv)
    weight, gain_sum = call(
        assemble, (sds((FEAT, CHAN), f32), sds((4, 128), f32)), 1, name="assemble"
    )(blocks.reshape(32, 4, 16, 128))
    return grad_obs, weight, gain_sum.reshape(CHAN)


def solution(mesh):
    return jax.shard_map(
        shards,
        mesh=mesh,
        in_specs=(
            P("tiles", None),
            P(None, "tiles"),
            P("tiles", None, None),
            P("tiles", None),
            P("tiles"),
            P("tiles", None),
            P(),
        ),
        out_specs=(P("tiles", None), P(), P()),
        check_vma=False,
    )
```

```python
import functools
import math

import jax
import jax.numpy as jnp
from jax import lax
from jax.experimental import pallas as pl
from jax.experimental.pallas import tpu as pltpu
from jax.sharding import PartitionSpec as P

f32, bf16 = jnp.float32, jnp.bfloat16
N_DEV = 128
CAP = 16
SLOTS = 2048
ROWS = 2048
FEAT = 256
CHAN = 512
CELLS = 4096
KAPPA = 1.0 / (2.0 * (0.375 * math.pi / 180.0) ** 2) / math.log(2.0)
VM = pl.BlockSpec(memory_space=pltpu.VMEM)


def call(body, out_shape, n_in, scratch=(), in_specs=None, name=None, limit=56, cost=None):
    many = isinstance(out_shape, (tuple, list))
    return pl.pallas_call(
        body,
        out_shape=out_shape,
        in_specs=in_specs or [VM] * n_in,
        out_specs=tuple(VM for _ in out_shape) if many else VM,
        scratch_shapes=list(scratch),
        compiler_params=pltpu.CompilerParams(vmem_limit_bytes=limit * 1024 * 1024),
        name=name,
        cost_estimate=cost,
    )


def cost(flops, nbytes):
    return pl.CostEstimate(flops=flops, bytes_accessed=nbytes, transcendentals=0)


def slot_major(x):
    lane = lax.broadcasted_iota(jnp.int32, (128, 128), 1) // 16
    sub = lax.broadcasted_iota(jnp.int32, (128, 128), 0) % 8
    y = jnp.where(lane == sub, jnp.concatenate([x] * 8, axis=1), jnp.zeros((), x.dtype))
    return jnp.sum(y.reshape(16, 8, 128), axis=1)


def gather_pos(rows_ref, count_ref, coords_ref, out_ref):
    slot = lax.broadcasted_iota(jnp.int32, (16, 128), 0)
    rows = jnp.where(slot < count_ref[...], rows_ref[...], -1)
    block, lane = rows >> 7, rows & 127
    pos = [jnp.zeros((16, 128), f32) for _ in range(3)]
    for t in range(ROWS // 128):
        hit = block == t
        for c in range(3):
            src = jnp.broadcast_to(coords_ref[c : c + 1, 128 * t : 128 * t + 128], (16, 128))
            got = jnp.take_along_axis(src, lane, axis=1, mode="promise_in_bounds")
            pos[c] = jnp.where(hit, got, pos[c])
    out_ref[...] = jnp.concatenate(pos + [jnp.zeros((80, 128), f32)], axis=0).T


def gather_feat(rows_ref, feat_ref, out_ref, rl_ref, hot_ref):
    x = jnp.concatenate([rows_ref[...].astype(f32), jnp.zeros((112, 128), f32)], axis=0).T
    rl = slot_major(x[:, 0:16])
    rl_ref[...] = rl.astype(jnp.int32)
    lane = lax.broadcasted_iota(jnp.int32, (128, 128), 1)
    for b in range(4):
        for q in range(4):
            r = 4 * b + q
            col = jnp.broadcast_to(rl[r : r + 1, :], (128, 128)).T.astype(jnp.int32)
            for t in range(ROWS // 128):
                hot_ref[128 * q : 128 * q + 128, 128 * t : 128 * t + 128] = jnp.where(
                    col == lane + 128 * t, 1.0, 0.0
                ).astype(bf16)
        out_ref[512 * b : 512 * b + 512, :] = jnp.dot(
            hot_ref[...], feat_ref[...], preferred_element_type=f32
        ).astype(bf16)


def adjoint_kernel(
    recv_ref, trig_ref, cot_hbm, adj_ref, gain_ref, c_ref, v_ref, m_ref, k_ref, w_ref, dens_ref, cot_ref, gacc_ref, sem
):
    load = pltpu.make_async_copy(cot_hbm, cot_ref, sem)
    load.start()
    cl, sl, cp, sp = [jnp.broadcast_to(trig_ref[:, i : i + 1], (64, 128)) for i in range(4)]
    c_ref[...] = cp
    x, y, z = [slot_major(recv_ref[:, 16 * c : 16 * c + 16]) for c in range(3)]
    for b in range(16):
        px, py, pz = x[b : b + 1, :], y[b : b + 1, :], z[b : b + 1, :]
        r2 = px * px + py * py
        inv = lax.rsqrt(jnp.maximum(r2, 1e-30))
        rho = r2 * inv
        cs = slice(128 * b, 128 * b + 128)
        v_ref[:, cs] = (-KAPPA * rho) * ((cl - px * inv) ** 2 + (sl - py * inv) ** 2)
        m_ref[:, cs] = -KAPPA * ((cp - rho) ** 2 + (sp - pz) ** 2)

    def group(g, _):
        base = pl.multiple_of(g * 8, 8)
        cc = c_ref[pl.ds(base, 8), :]
        rows = []
        for m in range(4):
            ds = []
            for h in range(2):
                i = 2 * m + h
                c = cc[i : i + 1, :]
                d = jnp.zeros((64, 128), f32)
                for b in range(16):
                    cs = slice(128 * b, 128 * b + 128)
                    mm = m_ref[pl.ds(base, 8), cs]
                    k = jnp.exp2(c * v_ref[:, cs] + mm[i : i + 1, :])
                    d = d + k
                    k_ref[pl.ds(pl.multiple_of(g * 512, 512) + 64 * i, 64), cs] = k.astype(bf16)
                ds.append(d)
            rows.append(jnp.sum(jnp.concatenate(ds, axis=0).T, axis=0, keepdims=True))
        dens_ref[g] = jnp.concatenate(rows, axis=0)
        return 0

    lax.fori_loop(0, 8, group, 0)
    load.wait()
    gacc_ref[...] = jnp.zeros_like(gacc_ref)

    def weigh(g, _):
        dens = dens_ref[g]
        scale = 1.0 / (1.0 + dens)
        logd = jnp.log1p(dens)
        for m in range(4):
            rs = pl.ds(pl.multiple_of(g * 512 + 128 * m, 128), 128)
            sc = jnp.broadcast_to(scale[m : m + 1, :], (128, 128)).T
            lg = jnp.broadcast_to(logd[m : m + 1, :], (128, 128)).T
            for q in range(4):
                cs = slice(128 * q, 128 * q + 128)
                x = cot_ref[rs, cs].astype(f32)
                w_ref[rs, cs] = (x * sc).astype(bf16)
                gacc_ref[:, cs] += jnp.sum((x * lg).reshape(16, 8, 128), axis=0)
        return 0

    lax.fori_loop(0, 8, weigh, 0)
    gain_ref[...] = jnp.sum(gacc_ref[...], axis=0, keepdims=True) * (1.0 / 2048.0)

    def slots(n, _):
        rs = pl.ds(pl.multiple_of(n * 512, 512), 512)
        adj_ref[rs, :] = lax.dot_general(
            k_ref[:, rs], w_ref[...], (((0,), (0,)), ((), ())), preferred_element_type=f32
        ).astype(bf16)
        return 0

    lax.fori_loop(0, SLOTS // 512, slots, 0)


def finish_tile(adj_ref, feat_ref, proj_ref, out_ref):
    for n in range(SLOTS // 512):
        s = lax.dot_general(
            adj_ref[512 * n : 512 * n + 512, :], proj_ref[...], (((1,), (1,)), ((), ())), preferred_element_type=f32
        ).astype(bf16)
        for h in range(2):
            t = s[:, 128 * h : 128 * h + 128]
            out_ref[8 * n : 8 * n + 8, :, 2 * h : 2 * h + 2] = t.reshape(8, 4, 2, 8, 128)
    w = lax.dot_general(feat_ref[...], adj_ref[...], (((0,), (0,)), ((), ())), preferred_element_type=f32)
    w = (w * (1.0 / 256.0)).astype(bf16)
    for cb in range(4):
        out_ref[:, cb, 4] = w[:, 128 * cb : 128 * cb + 128].reshape(32, 8, 128)


def reduce_block(recv_ref, gain_ref, out_ref):
    total = jnp.sum(recv_ref[:, 0].astype(f32), axis=0)
    g = jnp.concatenate([gain_ref[:, 128 * i : 128 * i + 128] for i in range(4)], axis=0)
    hi = g.astype(bf16).astype(f32)
    block = jnp.stack([total, jnp.concatenate([hi, g - hi], axis=0)]).astype(bf16)
    out_ref[...] = jnp.broadcast_to(block[None], (N_DEV, 2, 8, 128))


def scatter_rows(rl_ref, recv_ref, out_ref, val_ref, hot_ref):
    for h in range(2):
        val_ref[:, 128 * h : 128 * h + 128] = recv_ref[:, 2 * h : 2 * h + 2].reshape(SLOTS, 128)

    def rows(n, _):
        iota = lax.broadcasted_iota(jnp.int32, (512, 128), 0) + n * 512
        for b in range(16):
            hot_ref[:, 128 * b : 128 * b + 128] = jnp.where(iota == rl_ref[b : b + 1, :], 1.0, 0.0).astype(bf16)
        out_ref[pl.ds(pl.multiple_of(n * 512, 512), 512), :] = jnp.dot(
            hot_ref[...], val_ref[...], preferred_element_type=f32
        ).astype(bf16)
        return 0

    lax.fori_loop(0, ROWS // 512, rows, 0)


def assemble(x_ref, weight_ref, gain_ref):
    total = jnp.zeros((8, 128), f32)
    for cb in range(4):
        weight_ref[:, 128 * cb : 128 * cb + 128] = x_ref[:, cb, 0].astype(f32).reshape(256, 128)
        total = total + jnp.sum(x_ref[:, cb, 1].astype(f32), axis=0)
    gain_ref[...] = total[0:4] + total[4:8]


def trig_tables(tile):
    step = jnp.arange(64, dtype=f32)
    lat = (60.0 - ((tile // 16).astype(f32) * 64 + step + 0.5) * 0.25) * (math.pi / 180.0)
    lon = (-120.0 + ((tile % 16).astype(f32) * 64 + step + 0.5) * 0.25) * (math.pi / 180.0)
    return jnp.stack([jnp.cos(lon), jnp.sin(lon), jnp.cos(lat), jnp.sin(lat)], axis=1)


def exchange(x):
    return lax.all_to_all(x, "tiles", split_axis=0, concat_axis=0, tiled=True)


def shards(obs_feat, obs_coords, send_rows, send_count, tile_id, cotangent, projection):
    sds = jax.ShapeDtypeStruct
    rows = send_rows[0].T
    msg = call(gather_pos, sds((N_DEV, 128), f32), 3, name="gather_pos", limit=8)(rows, send_count, obs_coords)
    pos_in = exchange(msg.reshape(N_DEV, 1, 128)).reshape(N_DEV, 128)

    feat_out, rl = call(
        gather_feat,
        (sds((SLOTS, FEAT), bf16), sds((16, 128), jnp.int32)),
        2,
        scratch=[pltpu.VMEM((512, ROWS), bf16)],
        name="gather_feat",
        limit=16,
        cost=cost(4 * 10**9, 2 * 2**20),
    )(rows, obs_feat)
    trig = trig_tables(tile_id[0])

    feat_in = exchange(feat_out.reshape(N_DEV, CAP, FEAT)).reshape(SLOTS, FEAT)
    adj, gain = call(
        adjoint_kernel,
        (sds((SLOTS, CHAN), bf16), sds((1, CHAN), f32)),
        3,
        in_specs=[VM, VM, pl.BlockSpec(memory_space=pl.ANY)],
        scratch=[
            pltpu.VMEM((64, 128), f32),
            pltpu.VMEM((64, SLOTS), f32),
            pltpu.VMEM((64, SLOTS), f32),
            pltpu.VMEM((CELLS, SLOTS), bf16),
            pltpu.VMEM((CELLS, CHAN), bf16),
            pltpu.VMEM((8, 4, 128), f32),
            pltpu.VMEM((CELLS, CHAN), bf16),
            pltpu.VMEM((8, CHAN), f32),
            pltpu.SemaphoreType.DMA,
        ],
        name="adjoint",
        limit=48,
        cost=cost(20 * 10**9, 8 * 2**20),
    )(pos_in, trig, cotangent)

    out = call(finish_tile, sds((32, 4, 5, 8, 128), bf16), 3, name="finish_tile", limit=24)(adj, feat_in, projection)
    recv = exchange(out.reshape(N_DEV, 5, 8, 128))
    block = pl.pallas_call(
        reduce_block,
        grid=(1,),
        out_shape=sds((N_DEV, 2, 8, 128), bf16),
        in_specs=[pl.BlockSpec((N_DEV, 1, 8, 128), lambda i: (0, 4, 0, 0)), pl.BlockSpec((1, CHAN), lambda i: (0, 0))],
        out_specs=pl.BlockSpec((N_DEV, 2, 8, 128), lambda i: (0, 0, 0, 0)),
        name="reduce_block",
    )(recv, gain)
    blocks = exchange(block)
    grad_obs = call(
        scatter_rows,
        sds((ROWS, FEAT), bf16),
        2,
        scratch=[pltpu.VMEM((SLOTS, FEAT), bf16), pltpu.VMEM((512, SLOTS), bf16)],
        name="scatter_rows",
        limit=16,
        cost=cost(4 * 10**9, 3 * 2**20),
    )(rl, recv)
    weight, gain_sum = call(
        assemble, (sds((FEAT, CHAN), f32), sds((4, 128), f32)), 1, name="assemble", limit=8
    )(blocks.reshape(32, 4, 2, 8, 128))
    return grad_obs, weight, gain_sum.reshape(CHAN)


def solution(mesh):
    return jax.shard_map(
        shards,
        mesh=mesh,
        in_specs=(
            P("tiles", None),
            P(None, "tiles"),
            P("tiles", None, None),
            P("tiles", None),
            P("tiles"),
            P("tiles", None),
            P(),
        ),
        out_specs=(P("tiles", None), P(), P()),
        check_vma=False,
    )
```

```python
import functools
import math

import jax
import jax.numpy as jnp
from jax import lax
from jax.experimental import pallas as pl
from jax.experimental.pallas import tpu as pltpu
from jax.sharding import PartitionSpec as P

f32, bf16 = jnp.float32, jnp.bfloat16
N_DEV = 128
CAP = 16
SLOTS = 2048
ROWS = 2048
FEAT = 256
CHAN = 512
CELLS = 4096
KAPPA = 1.0 / (2.0 * (0.375 * math.pi / 180.0) ** 2) / math.log(2.0)
VM = pl.BlockSpec(memory_space=pltpu.VMEM)
HBM = pl.BlockSpec(memory_space=pltpu.HBM)
DMA = pltpu.SemaphoreType.DMA


def call(body, out_shape, n_in, scratch=(), in_specs=None, name=None, limit=24, cost=None):
    many = isinstance(out_shape, (tuple, list))
    return pl.pallas_call(
        body,
        out_shape=out_shape,
        in_specs=in_specs or [VM] * n_in,
        out_specs=tuple(VM for _ in out_shape) if many else VM,
        scratch_shapes=list(scratch),
        compiler_params=pltpu.CompilerParams(vmem_limit_bytes=int(limit * 1024 * 1024)),
        name=name,
        cost_estimate=cost,
    )


def cost(flops, nbytes):
    return pl.CostEstimate(flops=flops, bytes_accessed=nbytes, transcendentals=0)


def slot_major(x):
    lane = lax.broadcasted_iota(jnp.int32, (128, 128), 1) // 16
    sub = lax.broadcasted_iota(jnp.int32, (128, 128), 0) % 8
    y = jnp.where(lane == sub, jnp.concatenate([x] * 8, axis=1), jnp.zeros((), x.dtype))
    return jnp.sum(y.reshape(16, 8, 128), axis=1)


def load_all(pairs, sems):
    copies = [pltpu.make_async_copy(src, dst, sems.at[i]) for i, (src, dst) in enumerate(pairs)]
    for c in copies:
        c.start()
    return copies


def gather_pos(rows_hbm, count_hbm, coords_hbm, out_ref, rows_ref, count_ref, coords_ref, sems):
    for c in load_all([(rows_hbm, rows_ref), (count_hbm, count_ref), (coords_hbm, coords_ref)], sems):
        c.wait()
    slot = lax.broadcasted_iota(jnp.int32, (16, 128), 0)
    rows = jnp.where(slot < count_ref[...], rows_ref[...], -1)
    block, lane = rows >> 7, rows & 127
    pos = [jnp.zeros((16, 128), f32) for _ in range(3)]
    for t in range(ROWS // 128):
        hit = block == t
        for c in range(3):
            src = jnp.broadcast_to(coords_ref[c : c + 1, 128 * t : 128 * t + 128], (16, 128))
            got = jnp.take_along_axis(src, lane, axis=1, mode="promise_in_bounds")
            pos[c] = jnp.where(hit, got, pos[c])
    out_ref[...] = jnp.concatenate(pos + [jnp.zeros((80, 128), f32)], axis=0).T


def gather_feat(rows_hbm, feat_hbm, out_ref, rl_ref, hot_ref, rows_ref, feat_ref, sems):
    loads = load_all([(rows_hbm, rows_ref), (feat_hbm, feat_ref)], sems)
    loads[0].wait()
    x = jnp.concatenate([rows_ref[...].astype(f32), jnp.zeros((112, 128), f32)], axis=0).T
    rl = slot_major(x[:, 0:16])
    rl_ref[...] = rl.astype(jnp.int32)
    lane = lax.broadcasted_iota(jnp.int32, (128, 128), 1)
    for b in range(4):
        for q in range(4):
            r = 4 * b + q
            col = jnp.broadcast_to(rl[r : r + 1, :], (128, 128)).T.astype(jnp.int32)
            for t in range(ROWS // 128):
                hot_ref[128 * q : 128 * q + 128, 128 * t : 128 * t + 128] = jnp.where(
                    col == lane + 128 * t, 1.0, 0.0
                ).astype(bf16)
        if b == 0:
            loads[1].wait()
        out_ref[512 * b : 512 * b + 512, :] = jnp.dot(
            hot_ref[...], feat_ref[...], preferred_element_type=f32
        ).astype(bf16)


def adjoint_kernel(
    recv_ref, trig_ref, cot_hbm, adj_ref, gain_ref, c_ref, v_ref, m_ref, k_ref, w_ref, dens_ref, cot_ref, gacc_ref, sem
):
    load = pltpu.make_async_copy(cot_hbm, cot_ref, sem)
    load.start()
    cl, sl, cp, sp = [jnp.broadcast_to(trig_ref[:, i : i + 1], (64, 128)) for i in range(4)]
    c_ref[...] = cp
    x, y, z = [slot_major(recv_ref[:, 16 * c : 16 * c + 16]) for c in range(3)]
    for b in range(16):
        px, py, pz = x[b : b + 1, :], y[b : b + 1, :], z[b : b + 1, :]
        r2 = px * px + py * py
        inv = lax.rsqrt(jnp.maximum(r2, 1e-30))
        rho = r2 * inv
        cs = slice(128 * b, 128 * b + 128)
        v_ref[:, cs] = (-KAPPA * rho) * ((cl - px * inv) ** 2 + (sl - py * inv) ** 2)
        m_ref[:, cs] = -KAPPA * ((cp - rho) ** 2 + (sp - pz) ** 2)

    def group(g, _):
        base = pl.multiple_of(g * 8, 8)
        cc = c_ref[pl.ds(base, 8), :]
        rows = []
        for m in range(4):
            ds = []
            for h in range(2):
                i = 2 * m + h
                c = cc[i : i + 1, :]
                d = jnp.zeros((64, 128), f32)
                for b in range(16):
                    cs = slice(128 * b, 128 * b + 128)
                    mm = m_ref[pl.ds(base, 8), cs]
                    k = jnp.exp2(c * v_ref[:, cs] + mm[i : i + 1, :])
                    d = d + k
                    k_ref[pl.ds(pl.multiple_of(g * 512, 512) + 64 * i, 64), cs] = k.astype(bf16)
                ds.append(d)
            rows.append(jnp.sum(jnp.concatenate(ds, axis=0).T, axis=0, keepdims=True))
        dens_ref[g] = jnp.concatenate(rows, axis=0)
        return 0

    lax.fori_loop(0, 8, group, 0)
    load.wait()
    gacc_ref[...] = jnp.zeros_like(gacc_ref)

    def weigh(g, _):
        dens = dens_ref[g]
        scale = 1.0 / (1.0 + dens)
        logd = jnp.log1p(dens)
        for m in range(4):
            rs = pl.ds(pl.multiple_of(g * 512 + 128 * m, 128), 128)
            sc = jnp.broadcast_to(scale[m : m + 1, :], (128, 128)).T
            lg = jnp.broadcast_to(logd[m : m + 1, :], (128, 128)).T
            for q in range(4):
                cs = slice(128 * q, 128 * q + 128)
                x = cot_ref[rs, cs].astype(f32)
                w_ref[rs, cs] = (x * sc).astype(bf16)
                gacc_ref[:, cs] += jnp.sum((x * lg).reshape(16, 8, 128), axis=0)
        return 0

    lax.fori_loop(0, 8, weigh, 0)
    gain_ref[...] = jnp.sum(gacc_ref[...], axis=0, keepdims=True) * (1.0 / 2048.0)

    def slots(n, _):
        rs = pl.ds(pl.multiple_of(n * 1024, 1024), 1024)
        adj_ref[rs, :] = lax.dot_general(
            k_ref[:, rs], w_ref[...], (((0,), (0,)), ((), ())), preferred_element_type=f32
        ).astype(bf16)
        return 0

    lax.fori_loop(0, SLOTS // 1024, slots, 0)


def finish_tile(adj_ref, feat_ref, proj_hbm, out_ref, proj_ref, sems):
    load = load_all([(proj_hbm, proj_ref)], sems)[0]
    w = lax.dot_general(feat_ref[...], adj_ref[...], (((0,), (0,)), ((), ())), preferred_element_type=f32)
    w = (w * (1.0 / 256.0)).astype(bf16)
    for cb in range(4):
        out_ref[:, cb, 4] = w[:, 128 * cb : 128 * cb + 128].reshape(32, 8, 128)
    load.wait()
    for n in range(SLOTS // 512):
        s = lax.dot_general(
            adj_ref[512 * n : 512 * n + 512, :], proj_ref[...], (((1,), (1,)), ((), ())), preferred_element_type=f32
        ).astype(bf16)
        for h in range(2):
            t = s[:, 128 * h : 128 * h + 128]
            out_ref[8 * n : 8 * n + 8, :, 2 * h : 2 * h + 2] = t.reshape(8, 4, 2, 8, 128)


def reduce_block(recv_ref, gain_ref, out_ref):
    total = jnp.sum(recv_ref[:, 4].astype(f32), axis=0)
    g = jnp.concatenate([gain_ref[:, 128 * i : 128 * i + 128] for i in range(4)], axis=0)
    hi = g.astype(bf16).astype(f32)
    block = jnp.stack([total, jnp.concatenate([hi, g - hi], axis=0)]).astype(bf16)
    out_ref[...] = jnp.broadcast_to(block[None], (N_DEV, 2, 8, 128))


def scatter_rows(rl_ref, recv_ref, out_ref, val_ref, hot_ref):
    for h in range(2):
        val_ref[:, 128 * h : 128 * h + 128] = recv_ref[:, 2 * h : 2 * h + 2].reshape(SLOTS, 128)

    def rows(n, _):
        iota = lax.broadcasted_iota(jnp.int32, (512, 128), 0) + n * 512
        for b in range(16):
            hot_ref[:, 128 * b : 128 * b + 128] = jnp.where(iota == rl_ref[b : b + 1, :], 1.0, 0.0).astype(bf16)
        out_ref[pl.ds(pl.multiple_of(n * 512, 512), 512), :] = jnp.dot(
            hot_ref[...], val_ref[...], preferred_element_type=f32
        ).astype(bf16)
        return 0

    lax.fori_loop(0, ROWS // 512, rows, 0)


def assemble(x_ref, weight_ref, gain_ref):
    total = jnp.zeros((8, 128), f32)
    for cb in range(4):
        weight_ref[:, 128 * cb : 128 * cb + 128] = x_ref[:, cb, 0].astype(f32).reshape(256, 128)
        total = total + jnp.sum(x_ref[:, cb, 1].astype(f32), axis=0)
    gain_ref[...] = total[0:4] + total[4:8]


def trig_tables(tile):
    step = jnp.arange(64, dtype=f32)
    lat = (60.0 - ((tile // 16).astype(f32) * 64 + step + 0.5) * 0.25) * (math.pi / 180.0)
    lon = (-120.0 + ((tile % 16).astype(f32) * 64 + step + 0.5) * 0.25) * (math.pi / 180.0)
    return jnp.stack([jnp.cos(lon), jnp.sin(lon), jnp.cos(lat), jnp.sin(lat)], axis=1)


def exchange(x):
    return lax.all_to_all(x, "tiles", split_axis=0, concat_axis=0, tiled=True)


def shards(obs_feat, obs_coords, send_rows, send_count, tile_id, cotangent, projection):
    sds = jax.ShapeDtypeStruct
    rows = send_rows[0].T
    msg = call(
        gather_pos,
        sds((N_DEV, 128), f32),
        3,
        in_specs=[HBM] * 3,
        scratch=[pltpu.VMEM((CAP, N_DEV), jnp.int32), pltpu.VMEM((1, N_DEV), jnp.int32), pltpu.VMEM((3, ROWS), f32), DMA((3,))],
        name="gather_pos",
        limit=60.47,
    )(rows, send_count, obs_coords)
    pos_in = exchange(msg.reshape(N_DEV, 1, 128)).reshape(N_DEV, 128)

    feat_out, rl = call(
        gather_feat,
        (sds((SLOTS, FEAT), bf16), sds((16, 128), jnp.int32)),
        2,
        in_specs=[HBM] * 2,
        scratch=[pltpu.VMEM((512, ROWS), bf16), pltpu.VMEM((CAP, N_DEV), jnp.int32), pltpu.VMEM((ROWS, FEAT), bf16), DMA((2,))],
        name="gather_feat",
        limit=59,
        cost=cost(4 * 10**9, 2 * 2**20),
    )(rows, obs_feat)
    trig = trig_tables(tile_id[0])

    feat_in = exchange(feat_out.reshape(N_DEV, CAP, FEAT)).reshape(SLOTS, FEAT)
    adj, gain = call(
        adjoint_kernel,
        (sds((SLOTS, CHAN), bf16), sds((1, CHAN), f32)),
        3,
        in_specs=[VM, VM, HBM],
        scratch=[
            pltpu.VMEM((64, 128), f32),
            pltpu.VMEM((64, SLOTS), f32),
            pltpu.VMEM((64, SLOTS), f32),
            pltpu.VMEM((CELLS, SLOTS), bf16),
            pltpu.VMEM((CELLS, CHAN), bf16),
            pltpu.VMEM((8, 4, 128), f32),
            pltpu.VMEM((CELLS, CHAN), bf16),
            pltpu.VMEM((8, CHAN), f32),
            DMA,
        ],
        name="adjoint",
        limit=48,
        cost=cost(20 * 10**9, 8 * 2**20),
    )(pos_in, trig, cotangent)

    out = call(
        finish_tile,
        sds((32, 4, 5, 8, 128), bf16),
        3,
        in_specs=[VM, VM, HBM],
        scratch=[pltpu.VMEM((FEAT, CHAN), bf16), DMA((1,))],
        name="finish_tile",
        limit=24,
    )(adj, feat_in, projection)
    recv = exchange(out.reshape(N_DEV, 5, 8, 128))
    block = call(reduce_block, sds((N_DEV, 2, 8, 128), bf16), 2, name="reduce_block", limit=8)(recv, gain)
    blocks = exchange(block)
    grad_obs = call(
        scatter_rows,
        sds((ROWS, FEAT), bf16),
        2,
        scratch=[pltpu.VMEM((SLOTS, FEAT), bf16), pltpu.VMEM((512, SLOTS), bf16)],
        name="scatter_rows",
        limit=16,
        cost=cost(4 * 10**9, 3 * 2**20),
    )(rl, recv)
    weight, gain_sum = call(
        assemble, (sds((FEAT, CHAN), f32), sds((4, 128), f32)), 1, name="assemble", limit=8
    )(blocks.reshape(32, 4, 2, 8, 128))
    return grad_obs, weight, gain_sum.reshape(CHAN)


def solution(mesh):
    return jax.shard_map(
        shards,
        mesh=mesh,
        in_specs=(
            P("tiles", None),
            P(None, "tiles"),
            P("tiles", None, None),
            P("tiles", None),
            P("tiles"),
            P("tiles", None),
            P(),
        ),
        out_specs=(P("tiles", None), P(), P()),
        check_vma=False,
    )
```

```python
import functools
import math

import jax
import jax.numpy as jnp
from jax import lax
from jax.experimental import pallas as pl
from jax.experimental.pallas import tpu as pltpu
from jax.sharding import PartitionSpec as P

f32, bf16 = jnp.float32, jnp.bfloat16
N_DEV = 128
CAP = 16
SLOTS = 2048
ROWS = 2048
FEAT = 256
CHAN = 512
CELLS = 4096
KAPPA = 1.0 / (2.0 * (0.375 * math.pi / 180.0) ** 2) / math.log(2.0)
VM = pl.BlockSpec(memory_space=pltpu.VMEM)
HBM = pl.BlockSpec(memory_space=pltpu.HBM)
DMA = pltpu.SemaphoreType.DMA


def call(body, out_shape, n_in, scratch=(), in_specs=None, name=None, limit=24, cost=None):
    many = isinstance(out_shape, (tuple, list))
    return pl.pallas_call(
        body,
        out_shape=out_shape,
        in_specs=in_specs or [VM] * n_in,
        out_specs=tuple(VM for _ in out_shape) if many else VM,
        scratch_shapes=list(scratch),
        compiler_params=pltpu.CompilerParams(vmem_limit_bytes=int(limit * 1024 * 1024)),
        name=name,
        cost_estimate=cost,
    )


def cost(flops, nbytes):
    return pl.CostEstimate(flops=flops, bytes_accessed=nbytes, transcendentals=0)


def slot_major(x):
    lane = lax.broadcasted_iota(jnp.int32, (128, 128), 1) // 16
    sub = lax.broadcasted_iota(jnp.int32, (128, 128), 0) % 8
    y = jnp.where(lane == sub, jnp.concatenate([x] * 8, axis=1), jnp.zeros((), x.dtype))
    return jnp.sum(y.reshape(16, 8, 128), axis=1)


def load_all(pairs, sems):
    copies = [pltpu.make_async_copy(src, dst, sems.at[i]) for i, (src, dst) in enumerate(pairs)]
    for c in copies:
        c.start()
    return copies


def gather_pos(rows_hbm, count_hbm, coords_hbm, out_ref, rows_ref, count_ref, coords_ref, sems):
    for c in load_all([(rows_hbm, rows_ref), (count_hbm, count_ref), (coords_hbm, coords_ref)], sems):
        c.wait()
    slot = lax.broadcasted_iota(jnp.int32, (16, 128), 0)
    rows = jnp.where(slot < count_ref[...], rows_ref[...], -1)
    block, lane = rows >> 7, rows & 127
    pos = [jnp.zeros((16, 128), f32) for _ in range(3)]
    for t in range(ROWS // 128):
        hit = block == t
        for c in range(3):
            src = jnp.broadcast_to(coords_ref[c : c + 1, 128 * t : 128 * t + 128], (16, 128))
            got = jnp.take_along_axis(src, lane, axis=1, mode="promise_in_bounds")
            pos[c] = jnp.where(hit, got, pos[c])
    out_ref[...] = jnp.concatenate(pos + [jnp.zeros((80, 128), f32)], axis=0).T


def gather_feat(rows_hbm, feat_hbm, out_ref, rl_ref, hot_ref, rows_ref, feat_ref, sems):
    loads = load_all([(rows_hbm, rows_ref), (feat_hbm, feat_ref)], sems)
    loads[0].wait()
    x = jnp.concatenate([rows_ref[...].astype(f32), jnp.zeros((112, 128), f32)], axis=0).T
    rl = slot_major(x[:, 0:16])
    rl_ref[...] = rl.astype(jnp.int32)
    lane = lax.broadcasted_iota(jnp.int32, (128, 128), 1)
    for b in range(4):
        for q in range(4):
            r = 4 * b + q
            col = jnp.broadcast_to(rl[r : r + 1, :], (128, 128)).T.astype(jnp.int32)
            for t in range(ROWS // 128):
                hot_ref[128 * q : 128 * q + 128, 128 * t : 128 * t + 128] = jnp.where(
                    col == lane + 128 * t, 1.0, 0.0
                ).astype(bf16)
        if b == 0:
            loads[1].wait()
        out_ref[512 * b : 512 * b + 512, :] = jnp.dot(
            hot_ref[...], feat_ref[...], preferred_element_type=f32
        ).astype(bf16)


def adjoint_kernel(
    recv_ref, trig_ref, cot_hbm, adj_ref, gain_ref, c_ref, v_ref, m_ref, k_ref, w_ref, dens_ref, cot_ref, gacc_ref, sem
):
    load = pltpu.make_async_copy(cot_hbm, cot_ref, sem)
    load.start()
    cl, sl, cp, sp = [jnp.broadcast_to(trig_ref[:, i : i + 1], (64, 128)) for i in range(4)]
    c_ref[...] = cp
    x, y, z = [slot_major(recv_ref[:, 16 * c : 16 * c + 16]) for c in range(3)]
    for b in range(16):
        px, py, pz = x[b : b + 1, :], y[b : b + 1, :], z[b : b + 1, :]
        r2 = px * px + py * py
        inv = lax.rsqrt(jnp.maximum(r2, 1e-30))
        rho = r2 * inv
        cs = slice(128 * b, 128 * b + 128)
        v_ref[:, cs] = (-KAPPA * rho) * ((cl - px * inv) ** 2 + (sl - py * inv) ** 2)
        m_ref[:, cs] = -KAPPA * ((cp - rho) ** 2 + (sp - pz) ** 2)

    def group(g, _):
        base = pl.multiple_of(g * 8, 8)
        cc = c_ref[pl.ds(base, 8), :]
        rows = []
        for m in range(4):
            ds = []
            for h in range(2):
                i = 2 * m + h
                c = cc[i : i + 1, :]
                d = jnp.zeros((64, 128), f32)
                for b in range(16):
                    cs = slice(128 * b, 128 * b + 128)
                    mm = m_ref[pl.ds(base, 8), cs]
                    k = jnp.exp2(c * v_ref[:, cs] + mm[i : i + 1, :])
                    d = d + k
                    k_ref[pl.ds(pl.multiple_of(g * 512, 512) + 64 * i, 64), cs] = k.astype(bf16)
                ds.append(d)
            rows.append(jnp.sum(jnp.concatenate(ds, axis=0).T, axis=0, keepdims=True))
        dens_ref[g] = jnp.concatenate(rows, axis=0)
        return 0

    lax.fori_loop(0, 8, group, 0)
    load.wait()
    gacc_ref[...] = jnp.zeros_like(gacc_ref)

    def weigh(g, _):
        dens = dens_ref[g]
        scale = 1.0 / (1.0 + dens)
        logd = jnp.log1p(dens)
        for m in range(4):
            rs = pl.ds(pl.multiple_of(g * 512 + 128 * m, 128), 128)
            sc = jnp.broadcast_to(scale[m : m + 1, :], (128, 128)).T
            lg = jnp.broadcast_to(logd[m : m + 1, :], (128, 128)).T
            for q in range(4):
                cs = slice(128 * q, 128 * q + 128)
                x = cot_ref[rs, cs].astype(f32)
                w_ref[rs, cs] = (x * sc).astype(bf16)
                gacc_ref[:, cs] += jnp.sum((x * lg).reshape(16, 8, 128), axis=0)
        return 0

    lax.fori_loop(0, 8, weigh, 0, unroll=2)
    gain_ref[...] = jnp.sum(gacc_ref[...], axis=0, keepdims=True) * (1.0 / 2048.0)

    def slots(n, _):
        rs = pl.ds(pl.multiple_of(n * 1024, 1024), 1024)
        adj_ref[rs, :] = lax.dot_general(
            k_ref[:, rs], w_ref[...], (((0,), (0,)), ((), ())), preferred_element_type=f32
        ).astype(bf16)
        return 0

    lax.fori_loop(0, SLOTS // 1024, slots, 0)


def finish_tile(adj_ref, feat_ref, proj_hbm, out_ref, proj_ref, sems):
    load = load_all([(proj_hbm, proj_ref)], sems)[0]
    w = lax.dot_general(feat_ref[...], adj_ref[...], (((0,), (0,)), ((), ())), preferred_element_type=f32)
    w = (w * (1.0 / 256.0)).astype(bf16)
    for cb in range(4):
        out_ref[:, cb, 4] = w[:, 128 * cb : 128 * cb + 128].reshape(32, 8, 128)
    load.wait()
    for n in range(SLOTS // 512):
        s = lax.dot_general(
            adj_ref[512 * n : 512 * n + 512, :], proj_ref[...], (((1,), (1,)), ((), ())), preferred_element_type=f32
        ).astype(bf16)
        for h in range(2):
            t = s[:, 128 * h : 128 * h + 128]
            out_ref[8 * n : 8 * n + 8, :, 2 * h : 2 * h + 2] = t.reshape(8, 4, 2, 8, 128)


def reduce_block(recv_ref, gain_ref, out_ref):
    total = jnp.sum(recv_ref[:, 4].astype(f32), axis=0)
    g = [gain_ref[:, 128 * i : 128 * i + 128] for i in range(4)]
    block = jnp.concatenate([total] + g, axis=0).reshape(3, 4, 128).astype(bf16)
    out_ref[...] = jnp.broadcast_to(block[None], (N_DEV, 3, 4, 128))


def scatter_rows(rl_ref, recv_ref, out_ref, val_ref, hot_ref):
    for h in range(2):
        val_ref[:, 128 * h : 128 * h + 128] = recv_ref[:, 2 * h : 2 * h + 2].reshape(SLOTS, 128)

    def rows(n, _):
        iota = lax.broadcasted_iota(jnp.int32, (512, 128), 0) + n * 512
        for b in range(16):
            hot_ref[:, 128 * b : 128 * b + 128] = jnp.where(iota == rl_ref[b : b + 1, :], 1.0, 0.0).astype(bf16)
        out_ref[pl.ds(pl.multiple_of(n * 512, 512), 512), :] = jnp.dot(
            hot_ref[...], val_ref[...], preferred_element_type=f32
        ).astype(bf16)
        return 0

    lax.fori_loop(0, ROWS // 512, rows, 0)


def assemble(x_ref, weight_ref, gain_ref):
    total = jnp.zeros((4, 128), f32)
    for cb in range(4):
        weight_ref[:, 128 * cb : 128 * cb + 128] = x_ref[:, cb, 0:2].astype(f32).reshape(256, 128)
        total = total + jnp.sum(x_ref[:, cb, 2].astype(f32), axis=0)
    gain_ref[...] = total


def trig_tables(tile):
    step = jnp.arange(64, dtype=f32)
    lat = (60.0 - ((tile // 16).astype(f32) * 64 + step + 0.5) * 0.25) * (math.pi / 180.0)
    lon = (-120.0 + ((tile % 16).astype(f32) * 64 + step + 0.5) * 0.25) * (math.pi / 180.0)
    return jnp.stack([jnp.cos(lon), jnp.sin(lon), jnp.cos(lat), jnp.sin(lat)], axis=1)


def exchange(x):
    return lax.all_to_all(x, "tiles", split_axis=0, concat_axis=0, tiled=True)


def shards(obs_feat, obs_coords, send_rows, send_count, tile_id, cotangent, projection):
    sds = jax.ShapeDtypeStruct
    rows = send_rows[0].T
    msg = call(
        gather_pos,
        sds((N_DEV, 128), f32),
        3,
        in_specs=[HBM] * 3,
        scratch=[pltpu.VMEM((CAP, N_DEV), jnp.int32), pltpu.VMEM((1, N_DEV), jnp.int32), pltpu.VMEM((3, ROWS), f32), DMA((3,))],
        name="gather_pos",
        limit=60.47,
    )(rows, send_count, obs_coords)
    msg, tile_id = lax.optimization_barrier((msg, tile_id))
    pos_in = exchange(msg.reshape(N_DEV, 1, 128)).reshape(N_DEV, 128)

    feat_out, rl = call(
        gather_feat,
        (sds((SLOTS, FEAT), bf16), sds((16, 128), jnp.int32)),
        2,
        in_specs=[HBM] * 2,
        scratch=[pltpu.VMEM((512, ROWS), bf16), pltpu.VMEM((CAP, N_DEV), jnp.int32), pltpu.VMEM((ROWS, FEAT), bf16), DMA((2,))],
        name="gather_feat",
        limit=59,
        cost=cost(4 * 10**9, 2 * 2**20),
    )(rows, obs_feat)
    trig = trig_tables(tile_id[0])

    feat_in = exchange(feat_out.reshape(N_DEV, CAP, FEAT)).reshape(SLOTS, FEAT)
    adj, gain = call(
        adjoint_kernel,
        (sds((SLOTS, CHAN), bf16), sds((1, CHAN), f32)),
        3,
        in_specs=[VM, VM, HBM],
        scratch=[
            pltpu.VMEM((64, 128), f32),
            pltpu.VMEM((64, SLOTS), f32),
            pltpu.VMEM((64, SLOTS), f32),
            pltpu.VMEM((CELLS, SLOTS), bf16),
            pltpu.VMEM((CELLS, CHAN), bf16),
            pltpu.VMEM((8, 4, 128), f32),
            pltpu.VMEM((CELLS, CHAN), bf16),
            pltpu.VMEM((8, CHAN), f32),
            DMA,
        ],
        name="adjoint",
        limit=48,
        cost=cost(20 * 10**9, 8 * 2**20),
    )(pos_in, trig, cotangent)

    out = call(
        finish_tile,
        sds((32, 4, 5, 8, 128), bf16),
        3,
        in_specs=[VM, VM, HBM],
        scratch=[pltpu.VMEM((FEAT, CHAN), bf16), DMA((1,))],
        name="finish_tile",
        limit=24,
    )(adj, feat_in, projection)
    recv = exchange(out.reshape(N_DEV, 5, 8, 128))
    block = call(reduce_block, sds((N_DEV, 3, 4, 128), bf16), 2, name="reduce_block", limit=8)(recv, gain)
    blocks = exchange(block)
    grad_obs = call(
        scatter_rows,
        sds((ROWS, FEAT), bf16),
        2,
        scratch=[pltpu.VMEM((SLOTS, FEAT), bf16), pltpu.VMEM((512, SLOTS), bf16)],
        name="scatter_rows",
        limit=16,
        cost=cost(4 * 10**9, 3 * 2**20),
    )(rl, recv)
    weight, gain_sum = call(
        assemble, (sds((FEAT, CHAN), f32), sds((4, 128), f32)), 1, name="assemble", limit=8
    )(blocks.reshape(32, 4, 3, 4, 128))
    return grad_obs, weight, gain_sum.reshape(CHAN)


def solution(mesh):
    return jax.shard_map(
        shards,
        mesh=mesh,
        in_specs=(
            P("tiles", None),
            P(None, "tiles"),
            P("tiles", None, None),
            P("tiles", None),
            P("tiles"),
            P("tiles", None),
            P(),
        ),
        out_specs=(P("tiles", None), P(), P()),
        check_vma=False,
    )
```

```python
import functools
import math

import jax
import jax.numpy as jnp
from jax import lax
from jax.experimental import pallas as pl
from jax.experimental.pallas import tpu as pltpu
from jax.sharding import PartitionSpec as P

f32, bf16 = jnp.float32, jnp.bfloat16
N_DEV = 128
CAP = 16
SLOTS = 2048
ROWS = 2048
FEAT = 256
CHAN = 512
CELLS = 4096
KAPPA = 1.0 / (2.0 * (0.375 * math.pi / 180.0) ** 2) / math.log(2.0)
VM = pl.BlockSpec(memory_space=pltpu.VMEM)
HBM = pl.BlockSpec(memory_space=pltpu.HBM)
DMA = pltpu.SemaphoreType.DMA


def call(body, out_shape, n_in, scratch=(), in_specs=None, name=None, limit=24, cost=None):
    many = isinstance(out_shape, (tuple, list))
    return pl.pallas_call(
        body,
        out_shape=out_shape,
        in_specs=in_specs or [VM] * n_in,
        out_specs=tuple(VM for _ in out_shape) if many else VM,
        scratch_shapes=list(scratch),
        compiler_params=pltpu.CompilerParams(vmem_limit_bytes=int(limit * 1024 * 1024)),
        name=name,
        cost_estimate=cost,
    )


def cost(flops, nbytes):
    return pl.CostEstimate(flops=flops, bytes_accessed=nbytes, transcendentals=0)


def slot_major(x):
    lane = lax.broadcasted_iota(jnp.int32, (128, 128), 1) // 16
    sub = lax.broadcasted_iota(jnp.int32, (128, 128), 0) % 8
    y = jnp.where(lane == sub, jnp.concatenate([x] * 8, axis=1), jnp.zeros((), x.dtype))
    return jnp.sum(y.reshape(16, 8, 128), axis=1)


def load_all(pairs, sems):
    copies = [pltpu.make_async_copy(src, dst, sems.at[i]) for i, (src, dst) in enumerate(pairs)]
    for c in copies:
        c.start()
    return copies


def gather_pos(rows_hbm, count_hbm, coords_hbm, out_ref, rows_ref, count_ref, coords_ref, sems):
    for c in load_all([(rows_hbm, rows_ref), (count_hbm, count_ref), (coords_hbm, coords_ref)], sems):
        c.wait()
    slot = lax.broadcasted_iota(jnp.int32, (16, 128), 0)
    rows = jnp.where(slot < count_ref[...], rows_ref[...], -1)
    block, lane = rows >> 7, rows & 127
    pos = [jnp.zeros((16, 128), f32) for _ in range(3)]
    for t in range(ROWS // 128):
        hit = block == t
        for c in range(3):
            src = jnp.broadcast_to(coords_ref[c : c + 1, 128 * t : 128 * t + 128], (16, 128))
            got = jnp.take_along_axis(src, lane, axis=1, mode="promise_in_bounds")
            pos[c] = jnp.where(hit, got, pos[c])
    out_ref[...] = jnp.concatenate(pos + [jnp.zeros((80, 128), f32)], axis=0).T


def gather_feat(rows_hbm, feat_hbm, out_ref, rl_ref, hot_ref, rows_ref, feat_ref, sems):
    loads = load_all([(rows_hbm, rows_ref), (feat_hbm, feat_ref)], sems)
    loads[0].wait()
    x = jnp.concatenate([rows_ref[...].astype(f32), jnp.zeros((112, 128), f32)], axis=0).T
    rl = slot_major(x[:, 0:16])
    rl_ref[...] = rl.astype(jnp.int32)
    lane = lax.broadcasted_iota(jnp.int32, (128, 128), 1)
    for b in range(4):
        for q in range(4):
            r = 4 * b + q
            col = jnp.broadcast_to(rl[r : r + 1, :], (128, 128)).T.astype(jnp.int32)
            for t in range(ROWS // 128):
                hot_ref[128 * q : 128 * q + 128, 128 * t : 128 * t + 128] = jnp.where(
                    col == lane + 128 * t, 1.0, 0.0
                ).astype(bf16)
        if b == 0:
            loads[1].wait()
        out_ref[512 * b : 512 * b + 512, :] = jnp.dot(
            hot_ref[...], feat_ref[...], preferred_element_type=f32
        ).astype(bf16)


def adjoint_kernel(
    recv_ref, trig_ref, cot_hbm, adj_ref, gain_ref, c_ref, v_ref, m_ref, k_ref, w_ref, cot_ref, gacc_ref, sem
):
    def load(g):
        part = pl.ds(pl.multiple_of(g * 512, 512), 512)
        return pltpu.make_async_copy(cot_hbm.at[part], cot_ref.at[part], sem.at[g])

    for g in range(8):
        load(g).start()
    gacc_ref[...] = jnp.zeros_like(gacc_ref)
    cl, sl, cp, sp = [jnp.broadcast_to(trig_ref[:, i : i + 1], (64, 128)) for i in range(4)]
    c_ref[...] = cp
    x, y, z = [slot_major(recv_ref[:, 16 * c : 16 * c + 16]) for c in range(3)]
    for b in range(16):
        px, py, pz = x[b : b + 1, :], y[b : b + 1, :], z[b : b + 1, :]
        r2 = px * px + py * py
        inv = lax.rsqrt(jnp.maximum(r2, 1e-30))
        rho = r2 * inv
        cs = slice(128 * b, 128 * b + 128)
        v_ref[:, cs] = (-KAPPA * rho) * ((cl - px * inv) ** 2 + (sl - py * inv) ** 2)
        m_ref[:, cs] = -KAPPA * ((cp - rho) ** 2 + (sp - pz) ** 2)

    def columns(dens):
        sc = jnp.broadcast_to(1.0 / (1.0 + dens), (128, 128)).T
        lg = jnp.broadcast_to(jnp.log1p(dens), (128, 128)).T
        return sc, lg

    def weigh(row, q, sc, lg):
        rs = pl.ds(pl.multiple_of(row, 128), 128)
        cs = slice(128 * q, 128 * q + 128)
        x = cot_ref[rs, cs].astype(f32)
        w_ref[rs, cs] = (x * sc).astype(bf16)
        gacc_ref[:, cs] += jnp.sum((x * lg).reshape(16, 8, 128), axis=0)

    def group(g, dens):
        base = pl.multiple_of(g * 8, 8)
        before = jnp.maximum(g - 1, 0) * 512
        cc = c_ref[pl.ds(base, 8), :]
        rows = []
        for m in range(4):
            sc, lg = columns(dens[m : m + 1, :])
            ds = []
            for h in range(2):
                i = 2 * m + h
                c = cc[i : i + 1, :]
                d = jnp.zeros((64, 128), f32)
                for b in range(16):
                    cs = slice(128 * b, 128 * b + 128)
                    mm = m_ref[pl.ds(base, 8), cs]
                    k = jnp.exp2(c * v_ref[:, cs] + mm[i : i + 1, :])
                    d = d + k
                    k_ref[pl.ds(pl.multiple_of(g * 512, 512) + 64 * i, 64), cs] = k.astype(bf16)
                ds.append(d)
                weigh(before + 128 * m, 2 * h, sc, lg)
                weigh(before + 128 * m, 2 * h + 1, sc, lg)
            rows.append(jnp.sum(jnp.concatenate(ds, axis=0).T, axis=0, keepdims=True))

        @pl.when(g < 7)
        def _():
            load(g + 1).wait()

        return jnp.concatenate(rows, axis=0)

    load(0).wait()
    dens = lax.fori_loop(0, 8, group, jnp.zeros((4, 128), f32))
    for m in range(4):
        sc, lg = columns(dens[m : m + 1, :])
        for q in range(4):
            weigh(7 * 512 + 128 * m, q, sc, lg)
    gain_ref[...] = jnp.sum(gacc_ref[...], axis=0, keepdims=True) * (1.0 / 2048.0)

    def slots(n, _):
        rs = pl.ds(pl.multiple_of(n * 1024, 1024), 1024)
        adj_ref[rs, :] = lax.dot_general(
            k_ref[:, rs], w_ref[...], (((0,), (0,)), ((), ())), preferred_element_type=f32
        ).astype(bf16)
        return 0

    lax.fori_loop(0, SLOTS // 1024, slots, 0)


def finish_tile(adj_ref, feat_ref, proj_hbm, out_ref, proj_ref, sems):
    load = load_all([(proj_hbm, proj_ref)], sems)[0]
    w = lax.dot_general(feat_ref[...], adj_ref[...], (((0,), (0,)), ((), ())), preferred_element_type=f32)
    w = (w * (1.0 / 256.0)).astype(bf16)
    for cb in range(4):
        out_ref[:, cb, 4] = w[:, 128 * cb : 128 * cb + 128].reshape(32, 8, 128)
    load.wait()
    for n in range(SLOTS // 512):
        s = lax.dot_general(
            adj_ref[512 * n : 512 * n + 512, :], proj_ref[...], (((1,), (1,)), ((), ())), preferred_element_type=f32
        ).astype(bf16)
        for h in range(2):
            t = s[:, 128 * h : 128 * h + 128]
            out_ref[8 * n : 8 * n + 8, :, 2 * h : 2 * h + 2] = t.reshape(8, 4, 2, 8, 128)


def reduce_block(recv_ref, gain_ref, out_ref):
    total = jnp.sum(recv_ref[:, 4].astype(f32), axis=0)
    g = [gain_ref[:, 128 * i : 128 * i + 128] for i in range(4)]
    block = jnp.concatenate([total] + g, axis=0).reshape(3, 4, 128).astype(bf16)
    out_ref[...] = jnp.broadcast_to(block[None], (N_DEV, 3, 4, 128))


def scatter_rows(rl_ref, recv_ref, out_ref, val_ref, hot_ref):
    for h in range(2):
        val_ref[:, 128 * h : 128 * h + 128] = recv_ref[:, 2 * h : 2 * h + 2].reshape(SLOTS, 128)

    def rows(n, _):
        iota = lax.broadcasted_iota(jnp.int32, (512, 128), 0) + n * 512
        for b in range(16):
            hot_ref[:, 128 * b : 128 * b + 128] = jnp.where(iota == rl_ref[b : b + 1, :], 1.0, 0.0).astype(bf16)
        out_ref[pl.ds(pl.multiple_of(n * 512, 512), 512), :] = jnp.dot(
            hot_ref[...], val_ref[...], preferred_element_type=f32
        ).astype(bf16)
        return 0

    lax.fori_loop(0, ROWS // 512, rows, 0)


def assemble(x_ref, weight_ref, gain_ref):
    total = jnp.zeros((4, 128), f32)
    for cb in range(4):
        weight_ref[:, 128 * cb : 128 * cb + 128] = x_ref[:, cb, 0:2].astype(f32).reshape(256, 128)
        total = total + jnp.sum(x_ref[:, cb, 2].astype(f32), axis=0)
    gain_ref[...] = total


def trig_tables(tile):
    step = jnp.arange(64, dtype=f32)
    lat = (60.0 - ((tile // 16).astype(f32) * 64 + step + 0.5) * 0.25) * (math.pi / 180.0)
    lon = (-120.0 + ((tile % 16).astype(f32) * 64 + step + 0.5) * 0.25) * (math.pi / 180.0)
    return jnp.stack([jnp.cos(lon), jnp.sin(lon), jnp.cos(lat), jnp.sin(lat)], axis=1)


def exchange(x):
    return lax.all_to_all(x, "tiles", split_axis=0, concat_axis=0, tiled=True)


def shards(obs_feat, obs_coords, send_rows, send_count, tile_id, cotangent, projection):
    sds = jax.ShapeDtypeStruct
    rows = send_rows[0].T
    msg = call(
        gather_pos,
        sds((N_DEV, 128), f32),
        3,
        in_specs=[HBM] * 3,
        scratch=[pltpu.VMEM((CAP, N_DEV), jnp.int32), pltpu.VMEM((1, N_DEV), jnp.int32), pltpu.VMEM((3, ROWS), f32), DMA((3,))],
        name="gather_pos",
        limit=60.47,
    )(rows, send_count, obs_coords)
    msg, tile_id = lax.optimization_barrier((msg, tile_id))
    pos_in = exchange(msg.reshape(N_DEV, 1, 128)).reshape(N_DEV, 128)

    feat_out, rl = call(
        gather_feat,
        (sds((SLOTS, FEAT), bf16), sds((16, 128), jnp.int32)),
        2,
        in_specs=[HBM] * 2,
        scratch=[pltpu.VMEM((512, ROWS), bf16), pltpu.VMEM((CAP, N_DEV), jnp.int32), pltpu.VMEM((ROWS, FEAT), bf16), DMA((2,))],
        name="gather_feat",
        limit=59,
        cost=cost(4 * 10**9, 2 * 2**20),
    )(rows, obs_feat)
    trig = trig_tables(tile_id[0])

    feat_in = exchange(feat_out.reshape(N_DEV, CAP, FEAT)).reshape(SLOTS, FEAT)
    adj, gain = call(
        adjoint_kernel,
        (sds((SLOTS, CHAN), bf16), sds((1, CHAN), f32)),
        3,
        in_specs=[VM, VM, HBM],
        scratch=[
            pltpu.VMEM((64, 128), f32),
            pltpu.VMEM((64, SLOTS), f32),
            pltpu.VMEM((64, SLOTS), f32),
            pltpu.VMEM((CELLS, SLOTS), bf16),
            pltpu.VMEM((CELLS, CHAN), bf16),
            pltpu.VMEM((CELLS, CHAN), bf16),
            pltpu.VMEM((8, CHAN), f32),
            DMA((8,)),
        ],
        name="adjoint",
        limit=48,
        cost=cost(20 * 10**9, 8 * 2**20),
    )(pos_in, trig, cotangent)

    out = call(
        finish_tile,
        sds((32, 4, 5, 8, 128), bf16),
        3,
        in_specs=[VM, VM, HBM],
        scratch=[pltpu.VMEM((FEAT, CHAN), bf16), DMA((1,))],
        name="finish_tile",
        limit=24,
    )(adj, feat_in, projection)
    recv = exchange(out.reshape(N_DEV, 5, 8, 128))
    block = call(reduce_block, sds((N_DEV, 3, 4, 128), bf16), 2, name="reduce_block", limit=8)(recv, gain)
    blocks = exchange(block)
    grad_obs = call(
        scatter_rows,
        sds((ROWS, FEAT), bf16),
        2,
        scratch=[pltpu.VMEM((SLOTS, FEAT), bf16), pltpu.VMEM((512, SLOTS), bf16)],
        name="scatter_rows",
        limit=16,
        cost=cost(4 * 10**9, 3 * 2**20),
    )(rl, recv)
    weight, gain_sum = call(
        assemble, (sds((FEAT, CHAN), f32), sds((4, 128), f32)), 1, name="assemble", limit=8
    )(blocks.reshape(32, 4, 3, 4, 128))
    return grad_obs, weight, gain_sum.reshape(CHAN)


def solution(mesh):
    return jax.shard_map(
        shards,
        mesh=mesh,
        in_specs=(
            P("tiles", None),
            P(None, "tiles"),
            P("tiles", None, None),
            P("tiles", None),
            P("tiles"),
            P("tiles", None),
            P(),
        ),
        out_specs=(P("tiles", None), P(), P()),
        check_vma=False,
    )
```

```python
import functools
import math

import jax
import jax.numpy as jnp
from jax import lax
from jax.experimental import pallas as pl
from jax.experimental.pallas import tpu as pltpu
from jax.sharding import PartitionSpec as P

f32, bf16 = jnp.float32, jnp.bfloat16
N_DEV = 128
CAP = 16
SLOTS = 2048
ROWS = 2048
FEAT = 256
CHAN = 512
CELLS = 4096
KAPPA = 1.0 / (2.0 * (0.375 * math.pi / 180.0) ** 2) / math.log(2.0)
VM = pl.BlockSpec(memory_space=pltpu.VMEM)
HBM = pl.BlockSpec(memory_space=pltpu.HBM)
DMA = pltpu.SemaphoreType.DMA


def call(body, out_shape, n_in, scratch=(), in_specs=None, name=None, limit=24, cost=None):
    many = isinstance(out_shape, (tuple, list))
    return pl.pallas_call(
        body,
        out_shape=out_shape,
        in_specs=in_specs or [VM] * n_in,
        out_specs=tuple(VM for _ in out_shape) if many else VM,
        scratch_shapes=list(scratch),
        compiler_params=pltpu.CompilerParams(vmem_limit_bytes=int(limit * 1024 * 1024)),
        name=name,
        cost_estimate=cost,
    )


def cost(flops, nbytes):
    return pl.CostEstimate(flops=flops, bytes_accessed=nbytes, transcendentals=0)


def slot_major(x):
    lane = lax.broadcasted_iota(jnp.int32, (128, 128), 1) // 16
    sub = lax.broadcasted_iota(jnp.int32, (128, 128), 0) % 8
    y = jnp.where(lane == sub, jnp.concatenate([x] * 8, axis=1), jnp.zeros((), x.dtype))
    return jnp.sum(y.reshape(16, 8, 128), axis=1)


def load_all(pairs, sems):
    copies = [pltpu.make_async_copy(src, dst, sems.at[i]) for i, (src, dst) in enumerate(pairs)]
    for c in copies:
        c.start()
    return copies


def gather_pos(rows_hbm, count_hbm, coords_hbm, out_ref, rows_ref, count_ref, coords_ref, sems):
    for c in load_all([(rows_hbm, rows_ref), (count_hbm, count_ref), (coords_hbm, coords_ref)], sems):
        c.wait()
    slot = lax.broadcasted_iota(jnp.int32, (16, 128), 0)
    rows = jnp.where(slot < count_ref[...], rows_ref[...], -1)
    block, lane = rows >> 7, rows & 127
    pos = [jnp.zeros((16, 128), f32) for _ in range(3)]
    for t in range(ROWS // 128):
        hit = block == t
        for c in range(3):
            src = jnp.broadcast_to(coords_ref[c : c + 1, 128 * t : 128 * t + 128], (16, 128))
            got = jnp.take_along_axis(src, lane, axis=1, mode="promise_in_bounds")
            pos[c] = jnp.where(hit, got, pos[c])
    out_ref[...] = jnp.concatenate(pos + [jnp.zeros((80, 128), f32)], axis=0).T


def gather_feat(rows_hbm, feat_hbm, out_ref, rl_ref, hot_ref, rows_ref, feat_ref, sems):
    loads = load_all([(rows_hbm, rows_ref), (feat_hbm, feat_ref)], sems)
    loads[0].wait()
    x = jnp.concatenate([rows_ref[...].astype(f32), jnp.zeros((112, 128), f32)], axis=0).T
    rl = slot_major(x[:, 0:16])
    rl_ref[...] = rl.astype(jnp.int32)
    lane = lax.broadcasted_iota(jnp.int32, (128, 128), 1)
    for b in range(4):
        for q in range(4):
            r = 4 * b + q
            col = jnp.broadcast_to(rl[r : r + 1, :], (128, 128)).T.astype(jnp.int32)
            for t in range(ROWS // 128):
                hot_ref[128 * q : 128 * q + 128, 128 * t : 128 * t + 128] = jnp.where(
                    col == lane + 128 * t, 1.0, 0.0
                ).astype(bf16)
        if b == 0:
            loads[1].wait()
        out_ref[512 * b : 512 * b + 512, :] = jnp.dot(
            hot_ref[...], feat_ref[...], preferred_element_type=f32
        ).astype(bf16)


def adjoint_kernel(
    recv_ref, trig_ref, cot_hbm, adj_ref, gain_ref, c_ref, v_ref, m_ref, k_ref, w_ref, cot_ref, gacc_ref, sem
):
    def load(g):
        part = pl.ds(pl.multiple_of(g * 512, 512), 512)
        return pltpu.make_async_copy(cot_hbm.at[part], cot_ref.at[part], sem.at[g])

    for g in range(8):
        load(g).start()
    gacc_ref[...] = jnp.zeros_like(gacc_ref)
    cl, sl, cp, sp = [jnp.broadcast_to(trig_ref[:, i : i + 1], (64, 128)) for i in range(4)]
    c_ref[...] = cp
    x, y, z = [slot_major(recv_ref[:, 16 * c : 16 * c + 16]) for c in range(3)]
    for b in range(16):
        px, py, pz = x[b : b + 1, :], y[b : b + 1, :], z[b : b + 1, :]
        r2 = px * px + py * py
        inv = lax.rsqrt(jnp.maximum(r2, 1e-30))
        rho = r2 * inv
        cs = slice(128 * b, 128 * b + 128)
        v_ref[:, cs] = (-KAPPA * rho) * ((cl - px * inv) ** 2 + (sl - py * inv) ** 2)
        m_ref[:, cs] = -KAPPA * ((cp - rho) ** 2 + (sp - pz) ** 2)

    def columns(dens):
        sc = jnp.broadcast_to(1.0 / (1.0 + dens), (128, 128)).T
        lg = jnp.broadcast_to(jnp.log1p(dens), (128, 128)).T
        return sc, lg

    def weigh(row, q, sc, lg):
        rs = pl.ds(pl.multiple_of(row, 128), 128)
        cs = slice(128 * q, 128 * q + 128)
        x = cot_ref[rs, cs].astype(f32)
        w_ref[rs, cs] = (x * sc).astype(bf16)
        gacc_ref[:, cs] += jnp.sum((x * lg).reshape(16, 8, 128), axis=0)

    def group(g, dens):
        base = pl.multiple_of(g * 8, 8)
        before = (g - 1) * 512
        cc = c_ref[pl.ds(base, 8), :]
        rows = []
        for m in range(4):
            if dens is not None:
                sc, lg = columns(dens[m : m + 1, :])
            ds = []
            for h in range(2):
                i = 2 * m + h
                c = cc[i : i + 1, :]
                d = jnp.zeros((64, 128), f32)
                for b in range(16):
                    cs = slice(128 * b, 128 * b + 128)
                    mm = m_ref[pl.ds(base, 8), cs]
                    k = jnp.exp2(c * v_ref[:, cs] + mm[i : i + 1, :])
                    d = d + k
                    k_ref[pl.ds(pl.multiple_of(g * 512, 512) + 64 * i, 64), cs] = k.astype(bf16)
                ds.append(d)
                if dens is not None:
                    weigh(before + 128 * m, 2 * h, sc, lg)
                    weigh(before + 128 * m, 2 * h + 1, sc, lg)
            rows.append(jnp.sum(jnp.concatenate(ds, axis=0).T, axis=0, keepdims=True))
        load(g).wait()
        return jnp.concatenate(rows, axis=0)

    dens = lax.fori_loop(1, 8, group, group(0, None))
    for m in range(4):
        sc, lg = columns(dens[m : m + 1, :])
        for q in range(4):
            weigh(7 * 512 + 128 * m, q, sc, lg)
    gain_ref[...] = jnp.sum(gacc_ref[...], axis=0, keepdims=True) * (1.0 / 2048.0)

    def slots(n, _):
        rs = pl.ds(pl.multiple_of(n * 1024, 1024), 1024)
        adj_ref[rs, :] = lax.dot_general(
            k_ref[:, rs], w_ref[...], (((0,), (0,)), ((), ())), preferred_element_type=f32
        ).astype(bf16)
        return 0

    lax.fori_loop(0, SLOTS // 1024, slots, 0)


def finish_tile(adj_ref, feat_ref, proj_hbm, out_ref, proj_ref, sems):
    load = load_all([(proj_hbm, proj_ref)], sems)[0]
    w = lax.dot_general(feat_ref[...], adj_ref[...], (((0,), (0,)), ((), ())), preferred_element_type=f32)
    w = (w * (1.0 / 256.0)).astype(bf16)
    for cb in range(4):
        out_ref[:, cb, 4] = w[:, 128 * cb : 128 * cb + 128].reshape(32, 8, 128)
    load.wait()
    for n in range(SLOTS // 512):
        s = lax.dot_general(
            adj_ref[512 * n : 512 * n + 512, :], proj_ref[...], (((1,), (1,)), ((), ())), preferred_element_type=f32
        ).astype(bf16)
        for h in range(2):
            t = s[:, 128 * h : 128 * h + 128]
            out_ref[8 * n : 8 * n + 8, :, 2 * h : 2 * h + 2] = t.reshape(8, 4, 2, 8, 128)


def reduce_block(recv_ref, gain_ref, out_ref):
    total = jnp.sum(recv_ref[:, 4].astype(f32), axis=0)
    g = [gain_ref[:, 128 * i : 128 * i + 128] for i in range(4)]
    block = jnp.concatenate([total] + g, axis=0).reshape(3, 4, 128).astype(bf16)
    out_ref[...] = jnp.broadcast_to(block[None], (N_DEV, 3, 4, 128))


def scatter_rows(rl_ref, recv_ref, out_ref, val_ref, hot_ref):
    for h in range(2):
        val_ref[:, 128 * h : 128 * h + 128] = recv_ref[:, 2 * h : 2 * h + 2].reshape(SLOTS, 128)

    def rows(n, _):
        iota = lax.broadcasted_iota(jnp.int32, (512, 128), 0) + n * 512
        for b in range(16):
            hot_ref[:, 128 * b : 128 * b + 128] = jnp.where(iota == rl_ref[b : b + 1, :], 1.0, 0.0).astype(bf16)
        out_ref[pl.ds(pl.multiple_of(n * 512, 512), 512), :] = jnp.dot(
            hot_ref[...], val_ref[...], preferred_element_type=f32
        ).astype(bf16)
        return 0

    lax.fori_loop(0, ROWS // 512, rows, 0)


def assemble(x_ref, weight_ref, gain_ref):
    total = jnp.zeros((4, 128), f32)
    for cb in range(4):
        weight_ref[:, 128 * cb : 128 * cb + 128] = x_ref[:, cb, 0:2].astype(f32).reshape(256, 128)
        total = total + jnp.sum(x_ref[:, cb, 2].astype(f32), axis=0)
    gain_ref[...] = total


def trig_tables(tile):
    step = jnp.arange(64, dtype=f32)
    lat = (60.0 - ((tile // 16).astype(f32) * 64 + step + 0.5) * 0.25) * (math.pi / 180.0)
    lon = (-120.0 + ((tile % 16).astype(f32) * 64 + step + 0.5) * 0.25) * (math.pi / 180.0)
    return jnp.stack([jnp.cos(lon), jnp.sin(lon), jnp.cos(lat), jnp.sin(lat)], axis=1)


def exchange(x):
    return lax.all_to_all(x, "tiles", split_axis=0, concat_axis=0, tiled=True)


def shards(obs_feat, obs_coords, send_rows, send_count, tile_id, cotangent, projection):
    sds = jax.ShapeDtypeStruct
    rows = send_rows[0].T
    msg = call(
        gather_pos,
        sds((N_DEV, 128), f32),
        3,
        in_specs=[HBM] * 3,
        scratch=[pltpu.VMEM((CAP, N_DEV), jnp.int32), pltpu.VMEM((1, N_DEV), jnp.int32), pltpu.VMEM((3, ROWS), f32), DMA((3,))],
        name="gather_pos",
        limit=60.47,
    )(rows, send_count, obs_coords)
    msg, tile_id = lax.optimization_barrier((msg, tile_id))
    pos_in = exchange(msg.reshape(N_DEV, 1, 128)).reshape(N_DEV, 128)

    feat_out, rl = call(
        gather_feat,
        (sds((SLOTS, FEAT), bf16), sds((16, 128), jnp.int32)),
        2,
        in_specs=[HBM] * 2,
        scratch=[pltpu.VMEM((512, ROWS), bf16), pltpu.VMEM((CAP, N_DEV), jnp.int32), pltpu.VMEM((ROWS, FEAT), bf16), DMA((2,))],
        name="gather_feat",
        limit=59,
        cost=cost(4 * 10**9, 2 * 2**20),
    )(rows, obs_feat)
    trig = trig_tables(tile_id[0])

    feat_in = exchange(feat_out.reshape(N_DEV, CAP, FEAT)).reshape(SLOTS, FEAT)
    adj, gain = call(
        adjoint_kernel,
        (sds((SLOTS, CHAN), bf16), sds((1, CHAN), f32)),
        3,
        in_specs=[VM, VM, HBM],
        scratch=[
            pltpu.VMEM((64, 128), f32),
            pltpu.VMEM((64, SLOTS), f32),
            pltpu.VMEM((64, SLOTS), f32),
            pltpu.VMEM((CELLS, SLOTS), bf16),
            pltpu.VMEM((CELLS, CHAN), bf16),
            pltpu.VMEM((CELLS, CHAN), bf16),
            pltpu.VMEM((8, CHAN), f32),
            DMA((8,)),
        ],
        name="adjoint",
        limit=48,
        cost=cost(20 * 10**9, 8 * 2**20),
    )(pos_in, trig, cotangent)

    out = call(
        finish_tile,
        sds((32, 4, 5, 8, 128), bf16),
        3,
        in_specs=[VM, VM, HBM],
        scratch=[pltpu.VMEM((FEAT, CHAN), bf16), DMA((1,))],
        name="finish_tile",
        limit=24,
    )(adj, feat_in, projection)
    recv = exchange(out.reshape(N_DEV, 5, 8, 128))
    block = call(reduce_block, sds((N_DEV, 3, 4, 128), bf16), 2, name="reduce_block", limit=8)(recv, gain)
    blocks = exchange(block)
    grad_obs = call(
        scatter_rows,
        sds((ROWS, FEAT), bf16),
        2,
        scratch=[pltpu.VMEM((SLOTS, FEAT), bf16), pltpu.VMEM((512, SLOTS), bf16)],
        name="scatter_rows",
        limit=16,
        cost=cost(4 * 10**9, 3 * 2**20),
    )(rl, recv)
    weight, gain_sum = call(
        assemble, (sds((FEAT, CHAN), f32), sds((4, 128), f32)), 1, name="assemble", limit=8
    )(blocks.reshape(32, 4, 3, 4, 128))
    return grad_obs, weight, gain_sum.reshape(CHAN)


def solution(mesh):
    return jax.shard_map(
        shards,
        mesh=mesh,
        in_specs=(
            P("tiles", None),
            P(None, "tiles"),
            P("tiles", None, None),
            P("tiles", None),
            P("tiles"),
            P("tiles", None),
            P(),
        ),
        out_specs=(P("tiles", None), P(), P()),
        check_vma=False,
    )
```

```python
import functools
import math

import jax
import jax.numpy as jnp
from jax import lax
from jax.experimental import pallas as pl
from jax.experimental.pallas import tpu as pltpu
from jax.sharding import PartitionSpec as P

f32, bf16 = jnp.float32, jnp.bfloat16
N_DEV = 128
CAP = 16
SLOTS = 2048
ROWS = 2048
FEAT = 256
CHAN = 512
CELLS = 4096
KAPPA = 1.0 / (2.0 * (0.375 * math.pi / 180.0) ** 2) / math.log(2.0)
VM = pl.BlockSpec(memory_space=pltpu.VMEM)
HBM = pl.BlockSpec(memory_space=pltpu.HBM)
DMA = pltpu.SemaphoreType.DMA


def call(body, out_shape, n_in, scratch=(), in_specs=None, name=None, limit=24, cost=None):
    many = isinstance(out_shape, (tuple, list))
    return pl.pallas_call(
        body,
        out_shape=out_shape,
        in_specs=in_specs or [VM] * n_in,
        out_specs=tuple(VM for _ in out_shape) if many else VM,
        scratch_shapes=list(scratch),
        compiler_params=pltpu.CompilerParams(vmem_limit_bytes=int(limit * 1024 * 1024)),
        name=name,
        cost_estimate=cost,
    )


def cost(flops, nbytes):
    return pl.CostEstimate(flops=flops, bytes_accessed=nbytes, transcendentals=0)


def slot_major(x):
    lane = lax.broadcasted_iota(jnp.int32, (128, 128), 1) // 16
    sub = lax.broadcasted_iota(jnp.int32, (128, 128), 0) % 8
    y = jnp.where(lane == sub, jnp.concatenate([x] * 8, axis=1), jnp.zeros((), x.dtype))
    return jnp.sum(y.reshape(16, 8, 128), axis=1)


def load_all(pairs, sems):
    copies = [pltpu.make_async_copy(src, dst, sems.at[i]) for i, (src, dst) in enumerate(pairs)]
    for c in copies:
        c.start()
    return copies


def gather_pos(rows_hbm, count_hbm, coords_hbm, out_ref, rows_ref, count_ref, coords_ref, sems):
    for c in load_all([(rows_hbm, rows_ref), (count_hbm, count_ref), (coords_hbm, coords_ref)], sems):
        c.wait()
    slot = lax.broadcasted_iota(jnp.int32, (16, 128), 0)
    rows = jnp.where(slot < count_ref[...], rows_ref[...], -1)
    block, lane = rows >> 7, rows & 127
    pos = [jnp.zeros((16, 128), f32) for _ in range(3)]
    for t in range(ROWS // 128):
        hit = block == t
        for c in range(3):
            src = jnp.broadcast_to(coords_ref[c : c + 1, 128 * t : 128 * t + 128], (16, 128))
            got = jnp.take_along_axis(src, lane, axis=1, mode="promise_in_bounds")
            pos[c] = jnp.where(hit, got, pos[c])
    out_ref[...] = jnp.concatenate(pos + [jnp.zeros((80, 128), f32)], axis=0).T


def gather_feat(rows_hbm, feat_hbm, out_ref, rl_ref, hot_ref, rows_ref, feat_ref, sems):
    loads = load_all([(rows_hbm, rows_ref), (feat_hbm, feat_ref)], sems)
    loads[0].wait()
    x = jnp.concatenate([rows_ref[...].astype(f32), jnp.zeros((112, 128), f32)], axis=0).T
    rl = slot_major(x[:, 0:16])
    rl_ref[...] = rl.astype(jnp.int32)
    lane = lax.broadcasted_iota(jnp.int32, (128, 128), 1)
    for b in range(4):
        for q in range(4):
            r = 4 * b + q
            col = jnp.broadcast_to(rl[r : r + 1, :], (128, 128)).T.astype(jnp.int32)
            for t in range(ROWS // 128):
                hot_ref[128 * q : 128 * q + 128, 128 * t : 128 * t + 128] = jnp.where(
                    col == lane + 128 * t, 1.0, 0.0
                ).astype(bf16)
        if b == 0:
            loads[1].wait()
        out_ref[512 * b : 512 * b + 512, :] = jnp.dot(
            hot_ref[...], feat_ref[...], preferred_element_type=f32
        ).astype(bf16)


def adjoint_kernel(
    recv_ref, trig_ref, cot_hbm, proj_hbm, adj_ref, slot_ref, gain_ref,
    c_ref, v_ref, m_ref, k_ref, w_ref, cot_ref, gacc_ref, proj_ref, sem,
):
    def load(g):
        part = pl.ds(pl.multiple_of(g * 512, 512), 512)
        return pltpu.make_async_copy(cot_hbm.at[part], cot_ref.at[part], sem.at[g])

    for g in range(8):
        load(g).start()
    load_proj = pltpu.make_async_copy(proj_hbm, proj_ref, sem.at[8])
    load_proj.start()
    gacc_ref[...] = jnp.zeros_like(gacc_ref)
    cl, sl, cp, sp = [jnp.broadcast_to(trig_ref[:, i : i + 1], (64, 128)) for i in range(4)]
    c_ref[...] = cp
    x, y, z = [slot_major(recv_ref[:, 16 * c : 16 * c + 16]) for c in range(3)]
    for b in range(16):
        px, py, pz = x[b : b + 1, :], y[b : b + 1, :], z[b : b + 1, :]
        r2 = px * px + py * py
        inv = lax.rsqrt(jnp.maximum(r2, 1e-30))
        rho = r2 * inv
        cs = slice(128 * b, 128 * b + 128)
        v_ref[:, cs] = (-KAPPA * rho) * ((cl - px * inv) ** 2 + (sl - py * inv) ** 2)
        m_ref[:, cs] = -KAPPA * ((cp - rho) ** 2 + (sp - pz) ** 2)

    def columns(dens):
        sc = jnp.broadcast_to(1.0 / (1.0 + dens), (128, 128)).T
        lg = jnp.broadcast_to(jnp.log1p(dens), (128, 128)).T
        return sc, lg

    def weigh(row, q, sc, lg):
        rs = pl.ds(pl.multiple_of(row, 128), 128)
        cs = slice(128 * q, 128 * q + 128)
        x = cot_ref[rs, cs].astype(f32)
        w_ref[rs, cs] = (x * sc).astype(bf16)
        gacc_ref[:, cs] += jnp.sum((x * lg).reshape(16, 8, 128), axis=0)

    def group(g, dens):
        base = pl.multiple_of(g * 8, 8)
        before = (g - 1) * 512
        cc = c_ref[pl.ds(base, 8), :]
        rows = []
        for m in range(4):
            if dens is not None:
                sc, lg = columns(dens[m : m + 1, :])
            ds = []
            for h in range(2):
                i = 2 * m + h
                c = cc[i : i + 1, :]
                d = jnp.zeros((64, 128), f32)
                for b in range(16):
                    cs = slice(128 * b, 128 * b + 128)
                    mm = m_ref[pl.ds(base, 8), cs]
                    k = jnp.exp2(c * v_ref[:, cs] + mm[i : i + 1, :])
                    d = d + k
                    k_ref[pl.ds(pl.multiple_of(g * 512, 512) + 64 * i, 64), cs] = k.astype(bf16)
                ds.append(d)
                if dens is not None:
                    weigh(before + 128 * m, 2 * h, sc, lg)
                    weigh(before + 128 * m, 2 * h + 1, sc, lg)
            rows.append(jnp.sum(jnp.concatenate(ds, axis=0).T, axis=0, keepdims=True))
        load(g).wait()
        return jnp.concatenate(rows, axis=0)

    dens = lax.fori_loop(1, 8, group, group(0, None))
    for m in range(4):
        sc, lg = columns(dens[m : m + 1, :])
        for q in range(4):
            weigh(7 * 512 + 128 * m, q, sc, lg)
    gain_ref[...] = jnp.sum(gacc_ref[...], axis=0, keepdims=True) * (1.0 / 2048.0)

    load_proj.wait()

    def slots(n, _):
        rs = pl.ds(pl.multiple_of(n * 1024, 1024), 1024)
        a = lax.dot_general(
            k_ref[:, rs], w_ref[...], (((0,), (0,)), ((), ())), preferred_element_type=f32
        ).astype(bf16)
        adj_ref[rs, :] = a
        s = lax.dot_general(a, proj_ref[...], (((1,), (1,)), ((), ())), preferred_element_type=f32).astype(bf16)
        for h in range(2):
            part = s[:, 128 * h : 128 * h + 128].reshape(16, 4, 2, 8, 128)
            slot_ref[pl.ds(pl.multiple_of(n * 16, 16), 16), :, 2 * h : 2 * h + 2] = part
        return 0

    lax.fori_loop(0, SLOTS // 1024, slots, 0)


def finish_tile(adj_ref, slot_ref, feat_ref, out_ref):
    w = lax.dot_general(feat_ref[...], adj_ref[...], (((0,), (0,)), ((), ())), preferred_element_type=f32)
    out_ref[:, :, 0:4] = slot_ref[...]
    w = (w * (1.0 / 256.0)).astype(bf16)
    for cb in range(4):
        out_ref[:, cb, 4] = w[:, 128 * cb : 128 * cb + 128].reshape(32, 8, 128)


def reduce_block(recv_ref, gain_ref, out_ref):
    total = jnp.sum(recv_ref[:, 4].astype(f32), axis=0)
    g = [gain_ref[:, 128 * i : 128 * i + 128] for i in range(4)]
    block = jnp.concatenate([total] + g, axis=0).reshape(3, 4, 128).astype(bf16)
    out_ref[...] = jnp.broadcast_to(block[None], (N_DEV, 3, 4, 128))


def scatter_rows(rl_ref, recv_ref, out_ref, val_ref, hot_ref):
    for h in range(2):
        val_ref[:, 128 * h : 128 * h + 128] = recv_ref[:, 2 * h : 2 * h + 2].reshape(SLOTS, 128)

    def rows(n, _):
        iota = lax.broadcasted_iota(jnp.int32, (512, 128), 0) + n * 512
        for b in range(16):
            hot_ref[:, 128 * b : 128 * b + 128] = jnp.where(iota == rl_ref[b : b + 1, :], 1.0, 0.0).astype(bf16)
        out_ref[pl.ds(pl.multiple_of(n * 512, 512), 512), :] = jnp.dot(
            hot_ref[...], val_ref[...], preferred_element_type=f32
        ).astype(bf16)
        return 0

    lax.fori_loop(0, ROWS // 512, rows, 0)


def assemble(x_ref, weight_ref, gain_ref):
    total = jnp.zeros((4, 128), f32)
    for cb in range(4):
        weight_ref[:, 128 * cb : 128 * cb + 128] = x_ref[:, cb, 0:2].astype(f32).reshape(256, 128)
        total = total + jnp.sum(x_ref[:, cb, 2].astype(f32), axis=0)
    gain_ref[...] = total


def trig_tables(tile):
    step = jnp.arange(64, dtype=f32)
    lat = (60.0 - ((tile // 16).astype(f32) * 64 + step + 0.5) * 0.25) * (math.pi / 180.0)
    lon = (-120.0 + ((tile % 16).astype(f32) * 64 + step + 0.5) * 0.25) * (math.pi / 180.0)
    return jnp.stack([jnp.cos(lon), jnp.sin(lon), jnp.cos(lat), jnp.sin(lat)], axis=1)


def exchange(x):
    return lax.all_to_all(x, "tiles", split_axis=0, concat_axis=0, tiled=True)


def shards(obs_feat, obs_coords, send_rows, send_count, tile_id, cotangent, projection):
    sds = jax.ShapeDtypeStruct
    rows = send_rows[0].T
    msg = call(
        gather_pos,
        sds((N_DEV, 128), f32),
        3,
        in_specs=[HBM] * 3,
        scratch=[pltpu.VMEM((CAP, N_DEV), jnp.int32), pltpu.VMEM((1, N_DEV), jnp.int32), pltpu.VMEM((3, ROWS), f32), DMA((3,))],
        name="gather_pos",
        limit=60.47,
    )(rows, send_count, obs_coords)
    msg, tile_id = lax.optimization_barrier((msg, tile_id))
    pos_in = exchange(msg.reshape(N_DEV, 1, 128)).reshape(N_DEV, 128)

    feat_out, rl = call(
        gather_feat,
        (sds((SLOTS, FEAT), bf16), sds((16, 128), jnp.int32)),
        2,
        in_specs=[HBM] * 2,
        scratch=[pltpu.VMEM((512, ROWS), bf16), pltpu.VMEM((CAP, N_DEV), jnp.int32), pltpu.VMEM((ROWS, FEAT), bf16), DMA((2,))],
        name="gather_feat",
        limit=59,
        cost=cost(4 * 10**9, 2 * 2**20),
    )(rows, obs_feat)
    trig = trig_tables(tile_id[0])

    feat_in = exchange(feat_out.reshape(N_DEV, CAP, FEAT)).reshape(SLOTS, FEAT)
    adj, slot, gain = call(
        adjoint_kernel,
        (sds((SLOTS, CHAN), bf16), sds((32, 4, 4, 8, 128), bf16), sds((1, CHAN), f32)),
        4,
        in_specs=[VM, VM, HBM, HBM],
        scratch=[
            pltpu.VMEM((64, 128), f32),
            pltpu.VMEM((64, SLOTS), f32),
            pltpu.VMEM((64, SLOTS), f32),
            pltpu.VMEM((CELLS, SLOTS), bf16),
            pltpu.VMEM((CELLS, CHAN), bf16),
            pltpu.VMEM((CELLS, CHAN), bf16),
            pltpu.VMEM((8, CHAN), f32),
            pltpu.VMEM((FEAT, CHAN), bf16),
            DMA((9,)),
        ],
        name="adjoint",
        limit=48,
        cost=cost(20 * 10**9, 8 * 2**20),
    )(pos_in, trig, cotangent, projection)

    out = call(
        finish_tile,
        sds((32, 4, 5, 8, 128), bf16),
        3,
        name="finish_tile",
        limit=24,
    )(adj, slot, feat_in)
    recv = exchange(out.reshape(N_DEV, 5, 8, 128))
    block = call(reduce_block, sds((N_DEV, 3, 4, 128), bf16), 2, name="reduce_block", limit=8)(recv, gain)
    blocks = exchange(block)
    grad_obs = call(
        scatter_rows,
        sds((ROWS, FEAT), bf16),
        2,
        scratch=[pltpu.VMEM((SLOTS, FEAT), bf16), pltpu.VMEM((512, SLOTS), bf16)],
        name="scatter_rows",
        limit=16,
        cost=cost(4 * 10**9, 3 * 2**20),
    )(rl, recv)
    weight, gain_sum = call(
        assemble, (sds((FEAT, CHAN), f32), sds((4, 128), f32)), 1, name="assemble", limit=8
    )(blocks.reshape(32, 4, 3, 4, 128))
    return grad_obs, weight, gain_sum.reshape(CHAN)


def solution(mesh):
    return jax.shard_map(
        shards,
        mesh=mesh,
        in_specs=(
            P("tiles", None),
            P(None, "tiles"),
            P("tiles", None, None),
            P("tiles", None),
            P("tiles"),
            P("tiles", None),
            P(),
        ),
        out_specs=(P("tiles", None), P(), P()),
        check_vma=False,
    )
```

```python
import functools
import math

import jax
import jax.numpy as jnp
from jax import lax
from jax.experimental import pallas as pl
from jax.experimental.pallas import tpu as pltpu
from jax.sharding import PartitionSpec as P

f32, bf16 = jnp.float32, jnp.bfloat16
N_DEV = 128
CAP = 16
SLOTS = 2048
ROWS = 2048
FEAT = 256
CHAN = 512
CELLS = 4096
KAPPA = 1.0 / (2.0 * (0.375 * math.pi / 180.0) ** 2) / math.log(2.0)
VM = pl.BlockSpec(memory_space=pltpu.VMEM)
HBM = pl.BlockSpec(memory_space=pltpu.HBM)
DMA = pltpu.SemaphoreType.DMA


def call(body, out_shape, n_in, scratch=(), in_specs=None, out_specs=None, name=None, limit=24, cost=None):
    many = isinstance(out_shape, (tuple, list))
    return pl.pallas_call(
        body,
        out_shape=out_shape,
        in_specs=in_specs or [VM] * n_in,
        out_specs=out_specs or (tuple(VM for _ in out_shape) if many else VM),
        scratch_shapes=list(scratch),
        compiler_params=pltpu.CompilerParams(vmem_limit_bytes=int(limit * 1024 * 1024)),
        name=name,
        cost_estimate=cost,
    )


def cost(flops, nbytes):
    return pl.CostEstimate(flops=flops, bytes_accessed=nbytes, transcendentals=0)


def slot_major(x):
    lane = lax.broadcasted_iota(jnp.int32, (128, 128), 1) // 16
    sub = lax.broadcasted_iota(jnp.int32, (128, 128), 0) % 8
    y = jnp.where(lane == sub, jnp.concatenate([x] * 8, axis=1), jnp.zeros((), x.dtype))
    return jnp.sum(y.reshape(16, 8, 128), axis=1)


def load_all(pairs, sems):
    copies = [pltpu.make_async_copy(src, dst, sems.at[i]) for i, (src, dst) in enumerate(pairs)]
    for c in copies:
        c.start()
    return copies


def gather_pos(rows_hbm, count_hbm, coords_hbm, out_ref, rows_ref, count_ref, coords_ref, sems):
    for c in load_all([(rows_hbm, rows_ref), (count_hbm, count_ref), (coords_hbm, coords_ref)], sems):
        c.wait()
    slot = lax.broadcasted_iota(jnp.int32, (16, 128), 0)
    rows = jnp.where(slot < count_ref[...], rows_ref[...], -1)
    block, lane = rows >> 7, rows & 127
    pos = [jnp.zeros((16, 128), f32) for _ in range(3)]
    for t in range(ROWS // 128):
        hit = block == t
        for c in range(3):
            src = jnp.broadcast_to(coords_ref[c : c + 1, 128 * t : 128 * t + 128], (16, 128))
            got = jnp.take_along_axis(src, lane, axis=1, mode="promise_in_bounds")
            pos[c] = jnp.where(hit, got, pos[c])
    out_ref[...] = jnp.concatenate(pos + [jnp.zeros((80, 128), f32)], axis=0).T


def gather_feat(rows_hbm, feat_hbm, out_hbm, rl_ref, hot_ref, rows_ref, feat_ref, got_ref, sems):
    loads = load_all([(rows_hbm, rows_ref), (feat_hbm, feat_ref)], sems)
    loads[0].wait()
    x = jnp.concatenate([rows_ref[...].astype(f32), jnp.zeros((112, 128), f32)], axis=0).T
    rl = slot_major(x[:, 0:16])
    rl_ref[...] = rl.astype(jnp.int32)
    lane = lax.broadcasted_iota(jnp.int32, (128, 128), 1).astype(jnp.int16)
    stores = []
    for b in range(4):
        for q in range(4):
            r = 4 * b + q
            col = jnp.broadcast_to(rl[r : r + 1, :], (128, 128)).T.astype(jnp.int32).astype(jnp.int16)
            for t in range(ROWS // 128):
                hot_ref[b, 128 * q : 128 * q + 128, 128 * t : 128 * t + 128] = jnp.where(
                    col == lane + jnp.int16(128 * t), jnp.ones((), bf16), jnp.zeros((), bf16)
                )
        if b == 0:
            loads[1].wait()
        part = slice(512 * b, 512 * b + 512)
        got_ref[part] = jnp.dot(hot_ref[b], feat_ref[...], preferred_element_type=f32).astype(bf16)
        stores.append(pltpu.make_async_copy(got_ref.at[part], out_hbm.at[part], sems.at[2 + b]))
        stores[b].start()
    for c in stores:
        c.wait()


def adjoint_kernel(
    recv_ref, trig_ref, cot_hbm, adj_ref, gain_ref, c_ref, v_ref, m_ref, k_ref, w_ref, cot_ref, gacc_ref, sem
):
    def load(g):
        part = pl.ds(pl.multiple_of(g * 512, 512), 512)
        return pltpu.make_async_copy(cot_hbm.at[part], cot_ref.at[part], sem.at[g])

    for g in range(8):
        load(g).start()
    gacc_ref[...] = jnp.zeros_like(gacc_ref)
    cl, sl, cp, sp = [jnp.broadcast_to(trig_ref[:, i : i + 1], (64, 128)) for i in range(4)]
    c_ref[...] = cp
    x, y, z = [slot_major(recv_ref[:, 16 * c : 16 * c + 16]) for c in range(3)]
    for b in range(16):
        px, py, pz = x[b : b + 1, :], y[b : b + 1, :], z[b : b + 1, :]
        r2 = px * px + py * py
        inv = lax.rsqrt(jnp.maximum(r2, 1e-30))
        rho = r2 * inv
        cs = slice(128 * b, 128 * b + 128)
        v_ref[:, cs] = (-KAPPA * rho) * ((cl - px * inv) ** 2 + (sl - py * inv) ** 2)
        m_ref[:, cs] = -KAPPA * ((cp - rho) ** 2 + (sp - pz) ** 2)

    def columns(dens):
        sc = jnp.broadcast_to(1.0 / (1.0 + dens), (128, 128)).T
        lg = jnp.broadcast_to(jnp.log1p(dens), (128, 128)).T
        return sc, lg

    def weigh(row, q, sc, lg):
        rs = pl.ds(pl.multiple_of(row, 128), 128)
        cs = slice(128 * q, 128 * q + 128)
        x = cot_ref[rs, cs].astype(f32)
        w_ref[rs, cs] = (x * sc).astype(bf16)
        gacc_ref[:, cs] += jnp.sum((x * lg).reshape(16, 8, 128), axis=0)

    def group(g, dens):
        base = pl.multiple_of(g * 8, 8)
        before = (g - 1) * 512
        cc = c_ref[pl.ds(base, 8), :]
        rows = []
        for m in range(4):
            if dens is not None:
                sc, lg = columns(dens[m : m + 1, :])
            ds = []
            for h in range(2):
                i = 2 * m + h
                c = cc[i : i + 1, :]
                d = jnp.zeros((64, 128), f32)
                for b in range(16):
                    cs = slice(128 * b, 128 * b + 128)
                    mm = m_ref[pl.ds(base, 8), cs]
                    k = jnp.exp2(c * v_ref[:, cs] + mm[i : i + 1, :])
                    d = d + k
                    k_ref[pl.ds(pl.multiple_of(g * 512, 512) + 64 * i, 64), cs] = k.astype(bf16)
                ds.append(d)
                if dens is not None:
                    weigh(before + 128 * m, 2 * h, sc, lg)
                    weigh(before + 128 * m, 2 * h + 1, sc, lg)
            rows.append(jnp.sum(jnp.concatenate(ds, axis=0).T, axis=0, keepdims=True))
        load(g).wait()
        return jnp.concatenate(rows, axis=0)

    dens = lax.fori_loop(1, 8, group, group(0, None))
    for m in range(4):
        sc, lg = columns(dens[m : m + 1, :])
        for q in range(4):
            weigh(7 * 512 + 128 * m, q, sc, lg)
    gain_ref[...] = jnp.sum(gacc_ref[...], axis=0, keepdims=True) * (1.0 / 2048.0)

    def slots(n, _):
        rs = pl.ds(pl.multiple_of(n * 1024, 1024), 1024)
        adj_ref[rs, :] = lax.dot_general(
            k_ref[:, rs], w_ref[...], (((0,), (0,)), ((), ())), preferred_element_type=f32
        ).astype(bf16)
        return 0

    lax.fori_loop(0, SLOTS // 1024, slots, 0)


def finish_tile(adj_ref, feat_ref, proj_hbm, out_ref, proj_ref, sems):
    load = load_all([(proj_hbm, proj_ref)], sems)[0]
    w = lax.dot_general(feat_ref[...], adj_ref[...], (((0,), (0,)), ((), ())), preferred_element_type=f32)
    w = (w * (1.0 / 256.0)).astype(bf16)
    for cb in range(4):
        out_ref[:, cb, 4] = w[:, 128 * cb : 128 * cb + 128].reshape(32, 8, 128)
    load.wait()
    for n in range(SLOTS // 512):
        s = lax.dot_general(
            adj_ref[512 * n : 512 * n + 512, :], proj_ref[...], (((1,), (1,)), ((), ())), preferred_element_type=f32
        ).astype(bf16)
        for h in range(2):
            t = s[:, 128 * h : 128 * h + 128]
            out_ref[8 * n : 8 * n + 8, :, 2 * h : 2 * h + 2] = t.reshape(8, 4, 2, 8, 128)


def reduce_block(recv_ref, gain_ref, out_ref):
    total = jnp.sum(recv_ref[:, 4].astype(f32), axis=0)
    g = [gain_ref[:, 128 * i : 128 * i + 128] for i in range(4)]
    block = jnp.concatenate([total] + g, axis=0).reshape(3, 4, 128).astype(bf16)
    out_ref[...] = jnp.broadcast_to(block[None], (N_DEV, 3, 4, 128))


def scatter_rows(rl_ref, recv_ref, out_ref, val_ref, hot_ref):
    for h in range(2):
        val_ref[:, 128 * h : 128 * h + 128] = recv_ref[:, 2 * h : 2 * h + 2].reshape(SLOTS, 128)

    def rows(n, _):
        iota = lax.broadcasted_iota(jnp.int32, (512, 128), 0) + n * 512
        for b in range(16):
            hot_ref[:, 128 * b : 128 * b + 128] = jnp.where(iota == rl_ref[b : b + 1, :], 1.0, 0.0).astype(bf16)
        out_ref[pl.ds(pl.multiple_of(n * 512, 512), 512), :] = jnp.dot(
            hot_ref[...], val_ref[...], preferred_element_type=f32
        ).astype(bf16)
        return 0

    lax.fori_loop(0, ROWS // 512, rows, 0)


def assemble(x_ref, weight_ref, gain_ref):
    total = jnp.zeros((4, 128), f32)
    for cb in range(4):
        weight_ref[:, 128 * cb : 128 * cb + 128] = x_ref[:, cb, 0:2].astype(f32).reshape(256, 128)
        total = total + jnp.sum(x_ref[:, cb, 2].astype(f32), axis=0)
    gain_ref[...] = total


def trig_tables(tile):
    step = jnp.arange(64, dtype=f32)
    lat = (60.0 - ((tile // 16).astype(f32) * 64 + step + 0.5) * 0.25) * (math.pi / 180.0)
    lon = (-120.0 + ((tile % 16).astype(f32) * 64 + step + 0.5) * 0.25) * (math.pi / 180.0)
    return jnp.stack([jnp.cos(lon), jnp.sin(lon), jnp.cos(lat), jnp.sin(lat)], axis=1)


def exchange(x):
    return lax.all_to_all(x, "tiles", split_axis=0, concat_axis=0, tiled=True)


def shards(obs_feat, obs_coords, send_rows, send_count, tile_id, cotangent, projection):
    sds = jax.ShapeDtypeStruct
    rows = send_rows[0].T
    msg = call(
        gather_pos,
        sds((N_DEV, 128), f32),
        3,
        in_specs=[HBM] * 3,
        scratch=[pltpu.VMEM((CAP, N_DEV), jnp.int32), pltpu.VMEM((1, N_DEV), jnp.int32), pltpu.VMEM((3, ROWS), f32), DMA((3,))],
        name="gather_pos",
        limit=60.47,
    )(rows, send_count, obs_coords)
    msg, tile_id = lax.optimization_barrier((msg, tile_id))
    pos_in = exchange(msg.reshape(N_DEV, 1, 128)).reshape(N_DEV, 128)

    feat_out, rl = call(
        gather_feat,
        (sds((SLOTS, FEAT), bf16), sds((16, 128), jnp.int32)),
        2,
        in_specs=[HBM] * 2,
        out_specs=(HBM, VM),
        scratch=[
            pltpu.VMEM((4, 512, ROWS), bf16),
            pltpu.VMEM((CAP, N_DEV), jnp.int32),
            pltpu.VMEM((ROWS, FEAT), bf16),
            pltpu.VMEM((SLOTS, FEAT), bf16),
            DMA((6,)),
        ],
        name="gather_feat",
        limit=59,
        cost=cost(4 * 10**9, 2 * 2**20),
    )(rows, obs_feat)
    trig = trig_tables(tile_id[0])

    feat_in = exchange(feat_out.reshape(N_DEV, CAP, FEAT)).reshape(SLOTS, FEAT)
    adj, gain = call(
        adjoint_kernel,
        (sds((SLOTS, CHAN), bf16), sds((1, CHAN), f32)),
        3,
        in_specs=[VM, VM, HBM],
        scratch=[
            pltpu.VMEM((64, 128), f32),
            pltpu.VMEM((64, SLOTS), f32),
            pltpu.VMEM((64, SLOTS), f32),
            pltpu.VMEM((CELLS, SLOTS), bf16),
            pltpu.VMEM((CELLS, CHAN), bf16),
            pltpu.VMEM((CELLS, CHAN), bf16),
            pltpu.VMEM((8, CHAN), f32),
            DMA((8,)),
        ],
        name="adjoint",
        limit=48,
        cost=cost(20 * 10**9, 8 * 2**20),
    )(pos_in, trig, cotangent)

    out = call(
        finish_tile,
        sds((32, 4, 5, 8, 128), bf16),
        3,
        in_specs=[VM, VM, HBM],
        scratch=[pltpu.VMEM((FEAT, CHAN), bf16), DMA((1,))],
        name="finish_tile",
        limit=24,
    )(adj, feat_in, projection)
    recv = exchange(out.reshape(N_DEV, 5, 8, 128))
    block = call(reduce_block, sds((N_DEV, 3, 4, 128), bf16), 2, name="reduce_block", limit=8)(recv, gain)
    blocks = exchange(block)
    grad_obs = call(
        scatter_rows,
        sds((ROWS, FEAT), bf16),
        2,
        scratch=[pltpu.VMEM((SLOTS, FEAT), bf16), pltpu.VMEM((512, SLOTS), bf16)],
        name="scatter_rows",
        limit=16,
        cost=cost(4 * 10**9, 3 * 2**20),
    )(rl, recv)
    weight, gain_sum = call(
        assemble, (sds((FEAT, CHAN), f32), sds((4, 128), f32)), 1, name="assemble", limit=8
    )(blocks.reshape(32, 4, 3, 4, 128))
    return grad_obs, weight, gain_sum.reshape(CHAN)


def solution(mesh):
    return jax.shard_map(
        shards,
        mesh=mesh,
        in_specs=(
            P("tiles", None),
            P(None, "tiles"),
            P("tiles", None, None),
            P("tiles", None),
            P("tiles"),
            P("tiles", None),
            P(),
        ),
        out_specs=(P("tiles", None), P(), P()),
        check_vma=False,
    )
```

```python
import functools
import math

import jax
import jax.numpy as jnp
from jax import lax
from jax.experimental import pallas as pl
from jax.experimental.pallas import tpu as pltpu
from jax.sharding import PartitionSpec as P

f32, bf16 = jnp.float32, jnp.bfloat16
N_DEV = 128
CAP = 16
SLOTS = 2048
ROWS = 2048
FEAT = 256
CHAN = 512
CELLS = 4096
KAPPA = 1.0 / (2.0 * (0.375 * math.pi / 180.0) ** 2) / math.log(2.0)
VM = pl.BlockSpec(memory_space=pltpu.VMEM)
HBM = pl.BlockSpec(memory_space=pltpu.HBM)
DMA = pltpu.SemaphoreType.DMA


def call(body, out_shape, n_in, scratch=(), in_specs=None, out_specs=None, name=None, limit=24, cost=None):
    many = isinstance(out_shape, (tuple, list))
    return pl.pallas_call(
        body,
        out_shape=out_shape,
        in_specs=in_specs or [VM] * n_in,
        out_specs=out_specs or (tuple(VM for _ in out_shape) if many else VM),
        scratch_shapes=list(scratch),
        compiler_params=pltpu.CompilerParams(vmem_limit_bytes=int(limit * 1024 * 1024)),
        name=name,
        cost_estimate=cost,
    )


def cost(flops, nbytes):
    return pl.CostEstimate(flops=flops, bytes_accessed=nbytes, transcendentals=0)


def slot_major(x):
    lane = lax.broadcasted_iota(jnp.int32, (128, 128), 1) // 16
    sub = lax.broadcasted_iota(jnp.int32, (128, 128), 0) % 8
    y = jnp.where(lane == sub, jnp.concatenate([x] * 8, axis=1), jnp.zeros((), x.dtype))
    return jnp.sum(y.reshape(16, 8, 128), axis=1)


def load_all(pairs, sems):
    copies = [pltpu.make_async_copy(src, dst, sems.at[i]) for i, (src, dst) in enumerate(pairs)]
    for c in copies:
        c.start()
    return copies


def gather_pos(rows_hbm, count_hbm, coords_hbm, out_ref, rows_ref, count_ref, coords_ref, sems):
    for c in load_all([(rows_hbm, rows_ref), (count_hbm, count_ref), (coords_hbm, coords_ref)], sems):
        c.wait()
    slot = lax.broadcasted_iota(jnp.int32, (16, 128), 0)
    rows = jnp.where(slot < count_ref[...], rows_ref[...], -1)
    block, lane = rows >> 7, rows & 127
    pos = [jnp.zeros((16, 128), f32) for _ in range(3)]
    for t in range(ROWS // 128):
        hit = block == t
        for c in range(3):
            src = jnp.broadcast_to(coords_ref[c : c + 1, 128 * t : 128 * t + 128], (16, 128))
            got = jnp.take_along_axis(src, lane, axis=1, mode="promise_in_bounds")
            pos[c] = jnp.where(hit, got, pos[c])
    out_ref[...] = jnp.concatenate(pos + [jnp.zeros((80, 128), f32)], axis=0).T


def gather_feat(rows_hbm, feat_hbm, out_hbm, rl_ref, hot_ref, rows_ref, feat_ref, got_ref, sems):
    loads = load_all([(rows_hbm, rows_ref), (feat_hbm, feat_ref)], sems)
    loads[0].wait()
    x = jnp.concatenate([rows_ref[...].astype(f32), jnp.zeros((112, 128), f32)], axis=0).T
    rl = slot_major(x[:, 0:16])
    rl_ref[...] = rl.astype(jnp.int32)
    lane = lax.broadcasted_iota(jnp.int32, (128, 128), 1).astype(jnp.int16)
    stores = []
    for b in range(4):
        for q in range(4):
            r = 4 * b + q
            col = jnp.broadcast_to(rl[r : r + 1, :], (128, 128)).T.astype(jnp.int32).astype(jnp.int16)
            for t in range(ROWS // 128):
                hot_ref[b, 128 * q : 128 * q + 128, 128 * t : 128 * t + 128] = jnp.where(
                    col == lane + jnp.int16(128 * t), jnp.ones((), bf16), jnp.zeros((), bf16)
                )
        if b == 0:
            loads[1].wait()
        part = slice(512 * b, 512 * b + 512)
        got_ref[part] = jnp.dot(hot_ref[b], feat_ref[...], preferred_element_type=f32).astype(bf16)
        stores.append(pltpu.make_async_copy(got_ref.at[part], out_hbm.at[part], sems.at[2 + b]))
        stores[b].start()
    for c in stores:
        c.wait()


def adjoint_kernel(
    recv_ref, trig_ref, cot_hbm, adj_ref, gain_ref, c_ref, v_ref, m_ref, k_ref, w_ref, cot_ref, gacc_ref, sem
):
    def load(g):
        part = pl.ds(pl.multiple_of(g * 512, 512), 512)
        return pltpu.make_async_copy(cot_hbm.at[part], cot_ref.at[part], sem.at[g])

    for g in range(8):
        load(g).start()
    gacc_ref[...] = jnp.zeros_like(gacc_ref)
    cl, sl, cp, sp = [jnp.broadcast_to(trig_ref[:, i : i + 1], (64, 128)) for i in range(4)]
    c_ref[...] = cp
    x, y, z = [slot_major(recv_ref[:, 16 * c : 16 * c + 16]) for c in range(3)]
    for b in range(16):
        px, py, pz = x[b : b + 1, :], y[b : b + 1, :], z[b : b + 1, :]
        r2 = px * px + py * py
        inv = lax.rsqrt(jnp.maximum(r2, 1e-30))
        rho = r2 * inv
        cs = slice(128 * b, 128 * b + 128)
        v_ref[:, cs] = (-KAPPA * rho) * ((cl - px * inv) ** 2 + (sl - py * inv) ** 2)
        m_ref[:, cs] = -KAPPA * ((cp - rho) ** 2 + (sp - pz) ** 2)

    def columns(dens):
        sc = jnp.broadcast_to(1.0 / (1.0 + dens), (128, 128)).T
        lg = jnp.broadcast_to(jnp.log1p(dens), (128, 128)).T
        return sc, lg

    def weigh(row, q, sc, lg):
        rs = pl.ds(pl.multiple_of(row, 128), 128)
        cs = slice(128 * q, 128 * q + 128)
        x = cot_ref[rs, cs].astype(f32)
        w_ref[rs, cs] = (x * sc).astype(bf16)
        gacc_ref[:, cs] += jnp.sum((x * lg).reshape(16, 8, 128), axis=0)

    def group(g, dens):
        base = pl.multiple_of(g * 8, 8)
        before = (g - 1) * 512
        cc = c_ref[pl.ds(base, 8), :]
        rows = []
        for m in range(4):
            if dens is not None:
                sc, lg = columns(dens[m : m + 1, :])
            ds = []
            for h in range(2):
                i = 2 * m + h
                c = cc[i : i + 1, :]
                d = jnp.zeros((64, 128), f32)
                for b in range(16):
                    cs = slice(128 * b, 128 * b + 128)
                    mm = m_ref[pl.ds(base, 8), cs]
                    k = jnp.exp2(c * v_ref[:, cs] + mm[i : i + 1, :])
                    d = d + k
                    k_ref[pl.ds(pl.multiple_of(g * 512, 512) + 64 * i, 64), cs] = k.astype(bf16)
                ds.append(d)
                if dens is not None:
                    weigh(before + 128 * m, 2 * h, sc, lg)
                    weigh(before + 128 * m, 2 * h + 1, sc, lg)
            rows.append(jnp.sum(jnp.concatenate(ds, axis=0).T, axis=0, keepdims=True))
        load(g).wait()
        return jnp.concatenate(rows, axis=0)

    dens = lax.fori_loop(1, 8, group, group(0, None))
    for m in range(4):
        sc, lg = columns(dens[m : m + 1, :])
        for q in range(4):
            weigh(7 * 512 + 128 * m, q, sc, lg)
    gain_ref[...] = jnp.sum(gacc_ref[...], axis=0, keepdims=True) * (1.0 / 2048.0)

    adj_ref[...] = lax.dot_general(
        k_ref[...], w_ref[...], (((0,), (0,)), ((), ())), preferred_element_type=f32
    ).astype(bf16)


def finish_tile(adj_ref, feat_ref, proj_hbm, out_ref, proj_ref, sems):
    load = load_all([(proj_hbm, proj_ref)], sems)[0]
    w = lax.dot_general(feat_ref[...], adj_ref[...], (((0,), (0,)), ((), ())), preferred_element_type=f32)
    w = (w * (1.0 / 256.0)).astype(bf16)
    for cb in range(4):
        out_ref[:, cb, 4] = w[:, 128 * cb : 128 * cb + 128].reshape(32, 8, 128)
    load.wait()
    for n in range(SLOTS // 512):
        s = lax.dot_general(
            adj_ref[512 * n : 512 * n + 512, :], proj_ref[...], (((1,), (1,)), ((), ())), preferred_element_type=f32
        ).astype(bf16)
        for h in range(2):
            t = s[:, 128 * h : 128 * h + 128]
            out_ref[8 * n : 8 * n + 8, :, 2 * h : 2 * h + 2] = t.reshape(8, 4, 2, 8, 128)


def reduce_block(recv_ref, gain_ref, out_ref):
    total = jnp.sum(jnp.sum(recv_ref[:, 4].astype(f32).reshape(16, 8, 8, 128), axis=0), axis=0)
    g = [gain_ref[:, 128 * i : 128 * i + 128] for i in range(4)]
    block = jnp.concatenate([total] + g, axis=0).reshape(3, 4, 128).astype(bf16)
    out_ref[...] = jnp.broadcast_to(block[None], (N_DEV, 3, 4, 128))


def scatter_rows(rl_ref, recv_ref, out_ref, val_ref, hot_ref):
    for h in range(2):
        val_ref[:, 128 * h : 128 * h + 128] = recv_ref[:, 2 * h : 2 * h + 2].reshape(SLOTS, 128)

    def rows(n, _):
        iota = lax.broadcasted_iota(jnp.int32, (512, 128), 0) + n * 512
        for b in range(16):
            hot_ref[:, 128 * b : 128 * b + 128] = jnp.where(iota == rl_ref[b : b + 1, :], 1.0, 0.0).astype(bf16)
        out_ref[pl.ds(pl.multiple_of(n * 512, 512), 512), :] = jnp.dot(
            hot_ref[...], val_ref[...], preferred_element_type=f32
        ).astype(bf16)
        return 0

    lax.fori_loop(0, ROWS // 512, rows, 0)


def assemble(x_ref, weight_ref, gain_ref):
    total = jnp.zeros((4, 128), f32)
    for cb in range(4):
        weight_ref[:, 128 * cb : 128 * cb + 128] = x_ref[:, cb, 0:2].astype(f32).reshape(256, 128)
        total = total + jnp.sum(x_ref[:, cb, 2].astype(f32), axis=0)
    gain_ref[...] = total


def trig_tables(tile):
    step = jnp.arange(64, dtype=f32)
    lat = (60.0 - ((tile // 16).astype(f32) * 64 + step + 0.5) * 0.25) * (math.pi / 180.0)
    lon = (-120.0 + ((tile % 16).astype(f32) * 64 + step + 0.5) * 0.25) * (math.pi / 180.0)
    return jnp.stack([jnp.cos(lon), jnp.sin(lon), jnp.cos(lat), jnp.sin(lat)], axis=1)


def exchange(x):
    return lax.all_to_all(x, "tiles", split_axis=0, concat_axis=0, tiled=True)


def shards(obs_feat, obs_coords, send_rows, send_count, tile_id, cotangent, projection):
    sds = jax.ShapeDtypeStruct
    rows = send_rows[0].T
    msg = call(
        gather_pos,
        sds((N_DEV, 128), f32),
        3,
        in_specs=[HBM] * 3,
        scratch=[pltpu.VMEM((CAP, N_DEV), jnp.int32), pltpu.VMEM((1, N_DEV), jnp.int32), pltpu.VMEM((3, ROWS), f32), DMA((3,))],
        name="gather_pos",
        limit=60.47,
    )(rows, send_count, obs_coords)
    msg, tile_id = lax.optimization_barrier((msg, tile_id))
    pos_in = exchange(msg.reshape(N_DEV, 1, 128)).reshape(N_DEV, 128)

    feat_out, rl = call(
        gather_feat,
        (sds((SLOTS, FEAT), bf16), sds((16, 128), jnp.int32)),
        2,
        in_specs=[HBM] * 2,
        out_specs=(HBM, VM),
        scratch=[
            pltpu.VMEM((4, 512, ROWS), bf16),
            pltpu.VMEM((CAP, N_DEV), jnp.int32),
            pltpu.VMEM((ROWS, FEAT), bf16),
            pltpu.VMEM((SLOTS, FEAT), bf16),
            DMA((6,)),
        ],
        name="gather_feat",
        limit=59,
        cost=cost(4 * 10**9, 2 * 2**20),
    )(rows, obs_feat)
    trig = trig_tables(tile_id[0])

    feat_in = exchange(feat_out.reshape(N_DEV, CAP, FEAT)).reshape(SLOTS, FEAT)
    adj, gain = call(
        adjoint_kernel,
        (sds((SLOTS, CHAN), bf16), sds((1, CHAN), f32)),
        3,
        in_specs=[VM, VM, HBM],
        scratch=[
            pltpu.VMEM((64, 128), f32),
            pltpu.VMEM((64, SLOTS), f32),
            pltpu.VMEM((64, SLOTS), f32),
            pltpu.VMEM((CELLS, SLOTS), bf16),
            pltpu.VMEM((CELLS, CHAN), bf16),
            pltpu.VMEM((CELLS, CHAN), bf16),
            pltpu.VMEM((8, CHAN), f32),
            DMA((8,)),
        ],
        name="adjoint",
        limit=48,
        cost=cost(20 * 10**9, 8 * 2**20),
    )(pos_in, trig, cotangent)

    out = call(
        finish_tile,
        sds((32, 4, 5, 8, 128), bf16),
        3,
        in_specs=[VM, VM, HBM],
        scratch=[pltpu.VMEM((FEAT, CHAN), bf16), DMA((1,))],
        name="finish_tile",
        limit=24,
    )(adj, feat_in, projection)
    recv = exchange(out.reshape(N_DEV, 5, 8, 128))
    block = call(reduce_block, sds((N_DEV, 3, 4, 128), bf16), 2, name="reduce_block", limit=8)(recv, gain)
    blocks = exchange(block)
    grad_obs = call(
        scatter_rows,
        sds((ROWS, FEAT), bf16),
        2,
        scratch=[pltpu.VMEM((SLOTS, FEAT), bf16), pltpu.VMEM((512, SLOTS), bf16)],
        name="scatter_rows",
        limit=16,
        cost=cost(4 * 10**9, 3 * 2**20),
    )(rl, recv)
    weight, gain_sum = call(
        assemble, (sds((FEAT, CHAN), f32), sds((4, 128), f32)), 1, name="assemble", limit=8
    )(blocks.reshape(32, 4, 3, 4, 128))
    return grad_obs, weight, gain_sum.reshape(CHAN)


def solution(mesh):
    return jax.shard_map(
        shards,
        mesh=mesh,
        in_specs=(
            P("tiles", None),
            P(None, "tiles"),
            P("tiles", None, None),
            P("tiles", None),
            P("tiles"),
            P("tiles", None),
            P(),
        ),
        out_specs=(P("tiles", None), P(), P()),
        check_vma=False,
    )
```
